128 devices in a mesh: donor: 4 (over y), var: 32 (over z, x, core).
Axes of the slice: x: 4, y: 4, z: 4, core: 2. Of those that a mesh axis runs over, the one named last changes fastest.
Arguments:
- genotype: bfloat16 [10240, 131072], P('donor', 'var'), may hold values from -20 to 20
- block_place: int32 [1024], P('var'), may hold values from 0 to 1023, each once
- expression: bfloat16 [10240, 256], P('donor', 'var'), may hold values from -80 to 80
- covariates: bfloat16 [10240, 64], P('donor'), may hold values from -5 to 5
- gene_start: int32 [256], replicated, may hold values from -26 to 1023, as said below
- gene_count: int32 [256], replicated, may hold values from 1 to 52, as said below
- membership: float32 [256, 12288], P('var'), may hold values from 0 to 1
Outputs:
- gene_pvalue: float32 [256], P('var')
- pathway_pvalue: float32 [12288], P('var')
The draws below stay inside these ranges and needn't reach their ends.
Inputs may be any that keep to these rules, and one draw needn't show every extreme that they name: `block_place`: each genomic block is stored exactly once. gene_start[g] = 4 g - gene_count[g] // 2; window blocks outside 0 to 1023 hold no variants. `gene_count`: some gene has 52 blocks in every draw.
All inputs are finite; a program needn't handle non-finite values.
Results may differ from the reference program's by a relative error of at most 0.0057.
Values may be sent and summed in bfloat16 or wider, within the bound.
A program may use at most 192 MiB of HBM per device.

```python
import math
import jax
import jax.numpy as jnp
from jax import lax

VB = 128
BPG = 4
CMAX = 52
K = 64
DONORS = 10240
NBLK = 1024
VARIANTS = 131072
GENES = 256
GMAX = 14
PATHWAYS = 12288


def covariate_field(key):
    sub_key = jax.random.fold_in(key, 11)
    return jax.random.truncated_normal(sub_key, -5.0, 5.0, (DONORS, K), jnp.float32)


def window_fields(key):
    sub_key = jax.random.fold_in(key, 21)
    key_one, key_two, key_three, key_four = jax.random.split(sub_key, 4)
    factor_one = jax.random.randint(key_one, (GENES,), 0, CMAX)
    factor_two = jax.random.randint(key_two, (GENES,), 0, CMAX)
    extra_blocks = jax.random.randint(key_three, (GENES,), 0, CMAX // 6 + 1)
    window_count = jnp.minimum(1 + factor_one * factor_two // CMAX + extra_blocks, CMAX)
    chosen = jax.random.randint(key_four, (), 0, GENES)
    gene_index = jnp.arange(GENES, dtype=jnp.int32)
    window_count = jnp.where(gene_index == chosen, CMAX, window_count).astype(jnp.int32)
    window_start = (gene_index * BPG - window_count // 2).astype(jnp.int32)
    return (window_start, window_count)


def draw_covariates(key, part):
    shared = covariate_field(key)
    return shared.astype(jnp.bfloat16)


def draw_gene_start(key, part):
    window_start, window_count = window_fields(key)
    return window_start


def draw_gene_count(key, part):
    window_start, window_count = window_fields(key)
    return window_count


def draw_genotype(key, part):
    shared = covariate_field(key)
    key = jax.random.fold_in(key, 5)
    key_one, key_two, key_three = jax.random.split(key, 3)
    dosage = jax.random.uniform(key_one, (DONORS, VARIANTS), jnp.float32, -1.0, 1.0)
    loading_index = jax.random.randint(key_two, (12, VARIANTS), 0, K)
    loading = jnp.take(shared, loading_index[0], axis=1)
    for which in range(1, 12):
        loading = loading + jnp.take(shared, loading_index[which], axis=1)
    loading = jnp.clip(loading, -10.0, 10.0)
    spread = jnp.exp(jax.random.uniform(key_three, (VARIANTS,), jnp.float32, 0.0, math.log(10.0)))
    return (spread * (dosage + 0.08 * loading)).astype(jnp.bfloat16)


def draw_expression(key, part):
    shared = covariate_field(key)
    key = jax.random.fold_in(key, 7)
    key_one = jax.random.fold_in(key, 0)
    key_two = jax.random.fold_in(key, 1)
    key_four = jax.random.fold_in(key, 3)
    row_scale = jnp.exp(jax.random.uniform(key_one, (DONORS, 1), jnp.float32, 0.0, math.log(10.0)))
    loading_index = jax.random.randint(key_two, (GENES,), 0, K)
    noise_part = jax.random.truncated_normal(key_four, -5.0, 5.0, (DONORS, GENES), jnp.float32)
    return (row_scale * (noise_part + 0.3 * jnp.take(shared, loading_index, axis=1))).astype(jnp.bfloat16)


def draw_membership(key, part):
    key = jax.random.fold_in(key, 8)
    key_one, key_two = jax.random.split(key, 2)
    member_flag = jax.random.randint(key_one, (GENES, PATHWAYS), 0, max(GENES // 8, 4)) == 0
    weight_value = jax.random.uniform(key_two, (GENES, PATHWAYS), jnp.float32, 0.2, 1.0)
    return jnp.where(member_flag, weight_value, 0.0).astype(jnp.float32)


def setup_inputs(seed: int = 0) -> dict:
    key_list = jax.random.split(jax.random.key(seed), 8)
    genotype = draw_genotype(jax.random.fold_in(key_list[7], 71), 0)
    block_place = jax.random.permutation(key_list[1], NBLK).astype(jnp.int32)
    expression = draw_expression(jax.random.fold_in(key_list[7], 71), 0)
    covariates = draw_covariates(jax.random.fold_in(key_list[7], 71), 0)
    gene_start = draw_gene_start(jax.random.fold_in(key_list[7], 71), 0)
    gene_count = draw_gene_count(jax.random.fold_in(key_list[7], 71), 0)
    membership = draw_membership(jax.random.fold_in(key_list[7], 71), 0)
    return dict(genotype=genotype, block_place=block_place, expression=expression, covariates=covariates, gene_start=gene_start, gene_count=gene_count, membership=membership)


EPSILON = 1e-06

def cauchy_terms(zscore):
    angle_value = 0.5 * math.pi * lax.erfc(jnp.abs(zscore) * (1.0 / math.sqrt(2.0)))
    return jnp.sign(zscore) * jnp.cos(angle_value) / jnp.sin(angle_value)

def standardize(raw_values, covariates, cov_wide, gram_sum):
    cov_part = jnp.dot(covariates.T.astype(jnp.float32), raw_values.astype(jnp.float32), preferred_element_type=jnp.float32)
    beta_coef = jnp.linalg.solve(gram_sum, cov_part)
    residual = raw_values.astype(jnp.float32) - jnp.dot(cov_wide, beta_coef, precision=lax.Precision.HIGHEST)
    squares = lax.optimization_barrier(jnp.sum(residual * residual, axis=0))
    return (residual * lax.rsqrt(squares + EPSILON)).astype(jnp.bfloat16)

def reference(genotype, block_place, expression, covariates, gene_start, gene_count, membership):
    cov_wide = covariates.astype(jnp.float32)
    gram_sum = jnp.dot(covariates.T.astype(jnp.float32), covariates.astype(jnp.float32), preferred_element_type=jnp.float32)
    expr_std = standardize(expression, covariates, cov_wide, gram_sum)
    lead_blocks = CMAX - CMAX // 2 - 1
    scale_z = math.sqrt(DONORS - K - 2)
    offsets = jnp.arange(GMAX, dtype=jnp.int32)

    def one_block(stored):
        columns = lax.dynamic_slice_in_dim(genotype, stored * VB, VB, axis=1)
        geno_std = standardize(columns, covariates, cov_wide, gram_sum)
        logical = block_place[stored]
        slot_genes = (jnp.floor_divide(logical - lead_blocks, BPG) + offsets).astype(jnp.int32)
        inside = (slot_genes >= 0) & (slot_genes < GENES)
        safe_genes = jnp.clip(slot_genes, 0, GENES - 1)
        window_start = gene_start[safe_genes]
        window_count = gene_count[safe_genes]
        live_slots = inside & (window_start <= logical) & (logical < window_start + window_count)
        picked = jnp.take(expr_std, safe_genes, axis=1)
        correlation = jnp.dot(picked.T.astype(jnp.float32), geno_std.astype(jnp.float32), preferred_element_type=jnp.float32)
        slot_sums = lax.optimization_barrier(jnp.sum(cauchy_terms(correlation * scale_z), axis=1))
        return (jnp.where(live_slots, slot_sums, 0.0), safe_genes)
    slot_sums, slot_index = lax.map(one_block, jnp.arange(NBLK, dtype=jnp.int32))
    gene_sum = jnp.zeros((GENES,), jnp.float32).at[slot_index.reshape(-1)].add(slot_sums.reshape(-1))
    covered = jnp.minimum(gene_start + gene_count, NBLK) - jnp.maximum(gene_start, 0)
    gene_stat = gene_sum / (VB * covered).astype(jnp.float32)
    gene_pvalue = 0.5 - jnp.arctan(gene_stat) / math.pi
    member = membership.astype(jnp.float32)
    path_sum = jnp.dot(gene_stat, member, precision=lax.Precision.HIGHEST)
    path_weight = lax.optimization_barrier(jnp.sum(member, axis=0))
    pathway_pvalue = 0.5 - jnp.arctan(path_sum / jnp.maximum(path_weight, 1.0)) / math.pi
    return (gene_pvalue, pathway_pvalue)
```

```python
import math

import jax
import jax.numpy as jnp
from jax import lax
from jax.experimental import pallas as pl
from jax.experimental.pallas import tpu as pltpu
from jax.sharding import PartitionSpec as P

BPG = 4
CMAX = 52
K = 64
GMAX = 14
VB = 128
EPSILON = 1e-06
HIGHEST = lax.Precision.HIGHEST
MESH = pl.DeviceIdType.MESH
LEAD = CMAX - CMAX // 2 - 1
PAD = 8
ROWS = 72
TILE = 256


def cauchy_terms(zscore):
    angle_value = 0.5 * math.pi * lax.erfc(jnp.abs(zscore) * (1.0 / math.sqrt(2.0)))
    return jnp.sign(zscore) * jnp.cos(angle_value) / jnp.sin(angle_value)


def iota(shape, dim):
    return lax.broadcasted_iota(jnp.int32, shape, dim)


def sweep(pivot, mat):
    shape = mat.shape
    on_row = iota(shape, 0) == pivot
    on_col = iota(shape, 1) == pivot
    row = jnp.sum(jnp.where(on_row, mat, 0.0), axis=0, keepdims=True)
    col = jnp.sum(jnp.where(on_col, mat, 0.0), axis=1, keepdims=True)
    here = iota((shape[0], 1), 0) == pivot
    value = jnp.sum(jnp.where(here, col, 0.0), axis=0, keepdims=True)
    row = jnp.where(iota((1, shape[1]), 1) == pivot, 1.0, row) * (1.0 / value)
    col = jnp.where(here, 0.0, col)
    return jnp.where(on_row, row, jnp.where(on_col, 0.0, mat) - col * row)


def correlate(
    donors, groups, ce_ref, place_ref, x_ref, member_ref, out_ref, members_ref,
    xv, ct, ccc, small, inv_ref, cross_out, cross_in, beta, slab, expr_t, geno, pieces, wide, slot_out, slot_in,
    x_sem, small_sent, small_got, cross_sent, cross_got, beta_sent, beta_got,
    slab_sent, slab_got, member_sent, member_got, own_sem, slot_sent, slot_got,
):
    my_donor = lax.axis_index("donor")
    my_var = lax.axis_index("var")
    don_rows = ce_ref.shape[0]
    cols = xv.shape[2]
    tiles = cols // TILE
    chunks = don_rows // TILE
    paths = members_ref.shape[1]
    genes_here = member_ref.shape[0]
    half = slab.shape[2]

    def donor_at(step):
        return lax.rem(my_donor + step, donors)

    def var_at(step):
        return lax.rem(my_var + step, groups)

    def load(turn):
        start = pl.multiple_of(donor_at(1 + turn) * cols, cols)
        return pltpu.make_async_copy(x_ref.at[:, pl.ds(start, cols)], xv.at[turn], x_sem.at[turn])

    for turn in range(donors):
        load(turn).start()

    barrier = pltpu.get_barrier_semaphore()
    for step in range(1, donors):
        pl.semaphore_signal(
            barrier, inc=1, device_id=(donor_at(step), my_var), device_id_type=MESH
        )

    def greet(step, carry):
        pl.semaphore_signal(
            barrier, inc=1, device_id=(my_donor, var_at(step)), device_id_type=MESH
        )
        return carry

    lax.fori_loop(1, groups, greet, 0)

    eye = (iota((128, 128), 0) == iota((128, 128), 1)).astype(jnp.bfloat16)
    thrice = (iota((128, 256), 0) == lax.rem(iota((128, 256), 1), K)).astype(jnp.bfloat16)

    def prepare(chunk, total):
        rows = pl.ds(pl.multiple_of(chunk * TILE, TILE), TILE)
        part = ce_ref[rows, :]
        flipped = lax.dot_general(
            eye, part, (((1,), (1,)), ((), ())), preferred_element_type=jnp.float32
        ).astype(jnp.bfloat16)
        ct[:, rows] = flipped
        ccc[rows, :] = jnp.dot(part, thrice, preferred_element_type=jnp.float32).astype(
            jnp.bfloat16
        )
        return total + jnp.dot(flipped, part, preferred_element_type=jnp.float32)

    small[my_donor] = lax.fori_loop(0, chunks, prepare, jnp.zeros((128, 128), jnp.float32))
    pl.semaphore_wait(barrier, donors + groups - 2)

    def to_donor(step, src, dst, sent, got):
        return pltpu.make_async_remote_copy(
            src_ref=src,
            dst_ref=dst.at[my_donor],
            send_sem=sent.at[step],
            recv_sem=got.at[my_donor],
            device_id=(donor_at(step), my_var),
            device_id_type=MESH,
        )

    def from_donor(step, dst, sent, got):
        peer = donor_at(step)
        return pltpu.make_async_remote_copy(
            src_ref=dst.at[peer],
            dst_ref=dst.at[peer],
            send_sem=sent.at[step],
            recv_sem=got.at[peer],
            device_id=(peer, my_var),
            device_id_type=MESH,
        )

    for step in range(1, donors):
        to_donor(step, small.at[my_donor], small, small_sent, small_got).start()

    def member_copy(step):
        peer = var_at(step)
        return pltpu.make_async_remote_copy(
            src_ref=member_ref.at[:, pl.ds(pl.multiple_of(peer * paths, 128), paths)],
            dst_ref=members_ref.at[pl.ds(pl.multiple_of(my_var * genes_here, 8), genes_here), :],
            send_sem=member_sent.at[step],
            recv_sem=member_got.at[my_var],
            device_id=(my_donor, peer),
            device_id_type=MESH,
        )

    def member_back(step):
        peer = var_at(step)
        rows = members_ref.at[pl.ds(pl.multiple_of(peer * genes_here, 8), genes_here), :]
        return pltpu.make_async_remote_copy(
            src_ref=rows,
            dst_ref=rows,
            send_sem=member_sent.at[step],
            recv_sem=member_got.at[peer],
            device_id=(my_donor, peer),
            device_id_type=MESH,
        )

    def each(first, last, act):
        def body(step, carry):
            act(step)
            return carry

        lax.fori_loop(first, last, body, 0)

    each(1, groups, lambda step: member_copy(step).start())
    own_member = pltpu.make_async_copy(
        member_ref.at[:, pl.ds(pl.multiple_of(my_var * paths, 128), paths)],
        members_ref.at[pl.ds(pl.multiple_of(my_var * genes_here, 8), genes_here), :],
        own_sem,
    )
    own_member.start()

    wide[...] = jnp.zeros_like(wide)
    for step in range(1, donors):
        from_donor(step, small, small_sent, small_got).wait_recv()
    sums = small[0]
    for donor in range(1, donors):
        sums = sums + small[donor]

    def moments(turn, steps_done, sweeping):
        def body(index, carry):
            if sweeping:
                carry = sweep(steps_done + index, carry)
            tile = lax.div(index, chunks)
            chunk = lax.rem(index, chunks)
            rows = pl.ds(pl.multiple_of(chunk * TILE, TILE), TILE)
            lanes = pl.ds(pl.multiple_of(tile * TILE, TILE), TILE)
            part = xv[turn, rows, lanes]
            product = jnp.dot(ct[0:K, rows], part, preferred_element_type=jnp.float32)
            part = part.astype(jnp.float32)
            square = jnp.sum((part * part).reshape(TILE // 8, 8, TILE), axis=0)
            fresh = chunk == 0
            cross_out[turn, 0:K, lanes] = product + jnp.where(
                fresh, 0.0, cross_out[turn, 0:K, lanes]
            )
            cross_out[turn, K:ROWS, lanes] = square + jnp.where(
                fresh, 0.0, cross_out[turn, K:ROWS, lanes]
            )
            return carry

        return body

    mat = jnp.where(iota((K, 128), 1) < K, sums[0:K, :], 0.0)
    done = 0
    for turn in range(donors):
        load(turn).wait()
        now = min(K - done, tiles * chunks)
        mat = lax.fori_loop(0, now, moments(turn, done, True), mat)
        mat = lax.fori_loop(now, tiles * chunks, moments(turn, done, False), mat)
        done += now
        if turn < donors - 1:
            to_donor(turn + 1, cross_out.at[turn], cross_in, cross_sent, cross_got).start()
        else:
            cross_in[my_donor] = cross_out[turn]
    inv_ref[...] = mat
    inverse = inv_ref[:, 0:K]

    expr_rows = sums[K : K + 8, :]
    expr_coef = jnp.dot(
        expr_rows[:, 0:K], mat, precision=HIGHEST, preferred_element_type=jnp.float32
    )
    on_diag = iota((8, 128), 1) == iota((8, 128), 0) + K
    expr_sq = jnp.sum(jnp.where(on_diag, expr_rows, 0.0), axis=1, keepdims=True)
    in_cov = iota((8, 128), 1) < K
    expr_ss = expr_sq - jnp.sum(jnp.where(in_cov, expr_rows * expr_coef, 0.0), axis=1, keepdims=True)
    expr_scale = lax.rsqrt(jnp.maximum(expr_ss, 0.0) + EPSILON)
    mixing = jnp.where(in_cov, -expr_coef, jnp.where(on_diag, 1.0, 0.0))
    halves = []
    for part in range(2):
        resid = jnp.dot(
            mixing,
            ct[:, part * half : (part + 1) * half].astype(jnp.float32),
            precision=HIGHEST,
            preferred_element_type=jnp.float32,
        )
        halves.append(resid * expr_scale)
    slab[my_var] = jnp.concatenate(halves, axis=0).astype(jnp.bfloat16)

    def slab_copy(step):
        peer = var_at(step)
        return pltpu.make_async_remote_copy(
            src_ref=slab.at[my_var],
            dst_ref=slab.at[my_var],
            send_sem=slab_sent.at[step],
            recv_sem=slab_got.at[my_var],
            device_id=(my_donor, peer),
            device_id_type=MESH,
        )

    def slab_back(step):
        peer = var_at(step)
        return pltpu.make_async_remote_copy(
            src_ref=slab.at[peer],
            dst_ref=slab.at[peer],
            send_sem=slab_sent.at[step],
            recv_sem=slab_got.at[peer],
            device_id=(my_donor, peer),
            device_id_type=MESH,
        )

    each(1, groups, lambda step: slab_copy(step).start())

    for step in range(1, donors):
        from_donor(step, cross_in, cross_sent, cross_got).wait_recv()

    def solve(tile, carry):
        lanes = pl.ds(pl.multiple_of(tile * TILE, TILE), TILE)
        total = cross_in[0, :, lanes]
        for donor in range(1, donors):
            total = total + cross_in[donor, :, lanes]
        cross = total[0:K, :]
        square = jnp.sum(total[K:ROWS, :], axis=0, keepdims=True)
        coef = jnp.dot(
            inverse, cross, precision=HIGHEST, preferred_element_type=jnp.float32
        )
        left = square - jnp.sum(cross * coef, axis=0, keepdims=True)
        scale = lax.rsqrt(jnp.maximum(left, 0.0) + EPSILON)
        beta[my_donor, 0:K, lanes] = coef * scale
        beta[my_donor, K:ROWS, lanes] = jnp.broadcast_to(scale, (ROWS - K, TILE))
        return carry

    lax.fori_loop(0, tiles, solve, 0)
    for step in range(1, donors):
        to_donor(step, beta.at[my_donor], beta, beta_sent, beta_got).start()

    each(1, groups, lambda step: slab_back(step).wait_recv())
    per_copy = 4

    def unfold(index, carry):
        first = pl.multiple_of(index * per_copy, per_copy)
        part = slab[pl.ds(first, per_copy)].astype(jnp.float32)
        rows = pl.ds(pl.multiple_of(first * 8, per_copy * 8), per_copy * 8)
        expr_t[rows, 0:half] = part[:, 0:8, :].reshape(per_copy * 8, half).astype(jnp.bfloat16)
        expr_t[rows, half : 2 * half] = (
            part[:, 8:16, :].reshape(per_copy * 8, half).astype(jnp.bfloat16)
        )
        return carry

    lax.fori_loop(0, groups // per_copy, unfold, 0)

    def quarter(step):
        owner = donor_at(step)
        turn = (step + donors - 1) % donors

        def one_tile(tile, carry):
            lanes = pl.ds(pl.multiple_of(tile * TILE, TILE), TILE)
            coef = beta[owner, 0:K, lanes]
            scale = beta[owner, K : K + 1, lanes]
            for piece in range(3):
                rounded = coef.astype(jnp.bfloat16)
                pieces[piece * K : (piece + 1) * K, :] = rounded
                coef = coef - rounded.astype(jnp.float32)

            def standardize(chunk, inner):
                rows = pl.ds(pl.multiple_of(chunk * TILE, TILE), TILE)
                fitted = jnp.dot(
                    ccc[rows, 0 : 3 * K], pieces[...], preferred_element_type=jnp.float32
                )
                part = xv[turn, rows, lanes].astype(jnp.float32)
                geno[rows, :] = (part * scale - fitted).astype(jnp.bfloat16)
                return inner

            lax.fori_loop(0, chunks, standardize, 0)
            found = jnp.dot(expr_t[...], geno[...], preferred_element_type=jnp.float32)
            for side in range(TILE // VB):
                wide[side, PAD : PAD + expr_t.shape[0], :] = found[:, side * VB : (side + 1) * VB]
            for side in range(TILE // VB):
                block = tile * (TILE // VB) + side
                place = place_ref[owner * (cols // VB) + block]
                base = jnp.right_shift(place - LEAD, 2) + PAD
                found = wide[side, pl.ds(base, 16), :]
                if step:
                    slot_out[step, block] = found
                else:
                    slot_in[my_donor, block] = found
            return carry

        lax.fori_loop(0, tiles, one_tile, 0)

    for step in (0, 1, 3, 2):
        if step:
            from_donor(step, beta, beta_sent, beta_got).wait_recv()
        quarter(step)
        if step:
            to_donor(step, slot_out.at[step], slot_in, slot_sent, slot_got).start()

    for step in range(1, donors):
        from_donor(step, slot_in, slot_sent, slot_got).wait_recv()
    total = slot_in[0]
    for donor in range(1, donors):
        total = total + slot_in[donor]
    out_ref[...] = total

    own_member.wait()
    each(1, groups, lambda step: member_back(step).wait_recv())
    each(1, groups, lambda step: member_copy(step).wait_send())
    each(1, groups, lambda step: slab_copy(step).wait_send())
    for step in range(1, donors):
        to_donor(step, small.at[my_donor], small, small_sent, small_got).wait_send()
        to_donor(step, cross_out.at[step - 1], cross_in, cross_sent, cross_got).wait_send()
        to_donor(step, beta.at[my_donor], beta, beta_sent, beta_got).wait_send()
        to_donor(step, slot_out.at[step], slot_in, slot_sent, slot_got).wait_send()


def add_all(donors, groups, x_ref, out_ref, near, far, near_sent, near_got, far_sent, far_got):
    my_donor = lax.axis_index("donor")
    my_var = lax.axis_index("var")
    my_core = lax.rem(my_var, 2)
    my_chip = lax.div(my_var, 2)
    near_count, far_count = donors * 2, groups // 2
    my_near = my_donor * 2 + my_core

    def near_id(step):
        place = lax.rem(my_near + step, near_count)
        return place, (lax.div(place, 2), my_chip * 2 + lax.rem(place, 2))

    def far_id(step):
        place = lax.rem(my_chip + step, far_count)
        return place, (my_donor, place * 2 + my_core)

    barrier = pltpu.get_barrier_semaphore()
    for step in range(1, near_count):
        pl.semaphore_signal(barrier, inc=1, device_id=near_id(step)[1], device_id_type=MESH)
    for step in range(1, far_count):
        pl.semaphore_signal(barrier, inc=1, device_id=far_id(step)[1], device_id_type=MESH)
    near[my_near] = x_ref[...]
    pl.semaphore_wait(barrier, near_count + far_count - 2)

    for buffer, mine, count, where, sent, got in (
        (near, my_near, near_count, near_id, near_sent, near_got),
        (far, my_chip, far_count, far_id, far_sent, far_got),
    ):
        copies = []
        for step in range(1, count):
            copy = pltpu.make_async_remote_copy(
                src_ref=buffer.at[mine],
                dst_ref=buffer.at[mine],
                send_sem=sent.at[step],
                recv_sem=got.at[mine],
                device_id=where(step)[1],
                device_id_type=MESH,
            )
            copy.start()
            copies.append(copy)
        for step in range(1, count):
            peer, device = where(step)
            pltpu.make_async_remote_copy(
                src_ref=buffer.at[peer],
                dst_ref=buffer.at[peer],
                send_sem=sent.at[step],
                recv_sem=got.at[peer],
                device_id=device,
                device_id_type=MESH,
            ).wait_recv()
        total = buffer[0]
        for index in range(1, count):
            total = total + buffer[index]
        if buffer is near:
            far[my_chip] = total
        else:
            out_ref[...] = total
        for copy in copies:
            copy.wait_send()


def local(genotype, block_place, expression, covariates, gene_start, gene_count, membership):
    don_rows, var_cols = genotype.shape
    blocks_here = block_place.shape[0]
    block_width = var_cols // blocks_here
    genes_all = gene_start.shape[0]
    genes_here = expression.shape[1]
    groups = lax.axis_size("var")
    donors = lax.axis_size("donor")
    total_blocks = blocks_here * groups
    donors_all = don_rows * donors
    paths_here = membership.shape[1] // groups
    cols = var_cols // donors
    blocks_own = blocks_here // donors

    ce = jnp.concatenate(
        [
            covariates,
            expression,
            jnp.zeros((don_rows, 128 - K - genes_here), jnp.bfloat16),
        ],
        axis=1,
    )
    vmem = pl.BlockSpec(memory_space=pltpu.VMEM)
    anywhere = pl.BlockSpec(memory_space=pl.ANY)
    dma = pltpu.SemaphoreType.DMA

    def body(*refs):
        correlate(donors, groups, *refs)

    slots, members = pl.pallas_call(
        body,
        out_shape=(
            jax.ShapeDtypeStruct((blocks_own, 16, VB), jnp.float32),
            jax.ShapeDtypeStruct((genes_all, paths_here), jnp.float32),
        ),
        in_specs=[vmem, pl.BlockSpec(memory_space=pltpu.SMEM), anywhere, anywhere],
        out_specs=(vmem, vmem),
        scratch_shapes=[
            pltpu.VMEM((donors, don_rows, cols), jnp.bfloat16),
            pltpu.VMEM((128, don_rows), jnp.bfloat16),
            pltpu.VMEM((don_rows, 256), jnp.bfloat16),
            pltpu.VMEM((donors, 128, 128), jnp.float32),
            pltpu.VMEM((K, 128), jnp.float32),
            pltpu.VMEM((donors, ROWS, cols), jnp.float32),
            pltpu.VMEM((donors, ROWS, cols), jnp.float32),
            pltpu.VMEM((donors, ROWS, cols), jnp.float32),
            pltpu.VMEM((groups, 16, don_rows // 2), jnp.bfloat16),
            pltpu.VMEM((genes_all, don_rows), jnp.bfloat16),
            pltpu.VMEM((don_rows, TILE), jnp.bfloat16),
            pltpu.VMEM((3 * K, TILE), jnp.bfloat16),
            pltpu.VMEM((TILE // VB, genes_all + 24, VB), jnp.float32),
            pltpu.VMEM((donors, blocks_own, 16, VB), jnp.float32),
            pltpu.VMEM((donors, blocks_own, 16, VB), jnp.float32),
            dma((donors,)),
            *[dma((donors,)) for _ in range(6)],
            *[dma((groups,)) for _ in range(4)],
            dma,
            *[dma((donors,)) for _ in range(2)],
        ],
        compiler_params=pltpu.CompilerParams(
            collective_id=0, has_side_effects=True, vmem_limit_bytes=56 * 2**20
        ),
        name="correlate",
    )(ce, block_place, genotype, membership)

    place_own = lax.dynamic_slice_in_dim(
        block_place, lax.axis_index("donor") * blocks_own, blocks_own
    )
    offsets = jnp.arange(GMAX, dtype=jnp.int32)
    logical = place_own[:, None]
    slot_genes = jnp.floor_divide(logical - LEAD, BPG) + offsets[None, :]
    corr = slots[:, :GMAX, :]
    slot_sums = jnp.sum(cauchy_terms(corr * math.sqrt(donors_all - K - 2)), axis=2)
    genes = jnp.arange(genes_all, dtype=jnp.int32)
    hot = slot_genes[:, :, None] == genes
    live = (gene_start <= logical) & (logical < gene_start + gene_count)
    hot = hot & live[:, None, :]
    gene_part = jnp.sum(jnp.where(hot, slot_sums[:, :, None], 0.0), axis=(0, 1))

    def total_body(*refs):
        add_all(donors, groups, *refs)

    gene_sum = pl.pallas_call(
        total_body,
        out_shape=jax.ShapeDtypeStruct((genes_all // 128, 128), jnp.float32),
        in_specs=[vmem],
        out_specs=vmem,
        scratch_shapes=[
            pltpu.VMEM((donors * 2, genes_all // 128, 128), jnp.float32),
            pltpu.VMEM((groups // 2, genes_all // 128, 128), jnp.float32),
            dma((donors * 2,)),
            dma((donors * 2,)),
            dma((groups // 2,)),
            dma((groups // 2,)),
        ],
        compiler_params=pltpu.CompilerParams(collective_id=1, has_side_effects=True),
        name="add_all",
    )(gene_part.reshape(genes_all // 128, 128)).reshape(-1)

    covered = jnp.minimum(gene_start + gene_count, total_blocks) - jnp.maximum(gene_start, 0)
    gene_stat = gene_sum / (block_width * covered).astype(jnp.float32)
    own_stat = lax.dynamic_slice_in_dim(
        gene_stat, lax.axis_index("var") * genes_here, genes_here
    )
    gene_pvalue = 0.5 - jnp.arctan(own_stat) / math.pi
    path_sum = jnp.dot(gene_stat, members, precision=HIGHEST)
    path_weight = jnp.sum(members, axis=0)
    pathway_pvalue = 0.5 - jnp.arctan(path_sum / jnp.maximum(path_weight, 1.0)) / math.pi
    return (gene_pvalue, pathway_pvalue)


def solution(mesh):
    placed = (
        P("donor", "var"),
        P("var"),
        P("donor", "var"),
        P("donor", None),
        P(),
        P(),
        P("var", None),
    )
    return jax.shard_map(
        local, mesh=mesh, in_specs=placed, out_specs=(P("var"), P("var")), check_vma=False
    )
```

```python
import math

import jax
import jax.numpy as jnp
from jax import lax
from jax.experimental import pallas as pl
from jax.experimental.pallas import tpu as pltpu
from jax.sharding import PartitionSpec as P

BPG = 4
CMAX = 52
K = 64
GMAX = 14
VB = 128
EPSILON = 1e-06
HIGHEST = lax.Precision.HIGHEST
MESH = pl.DeviceIdType.MESH
LEAD = CMAX - CMAX // 2 - 1
PAD = 8
ROWS = 72
TILE = 256
STRIP = 512


SIN = (1.6059043837e-10, -2.5052108385e-8, 2.7557319224e-6, -1.9841269841e-4, 8.3333333333e-3, -1.6666666667e-1, 1.0)
COS = (-1.1470745598e-11, 2.0876756988e-9, -2.7557319224e-7, 2.4801587302e-5, -1.3888888889e-3, 4.1666666667e-2, -0.5, 1.0)
ERF = (7.853861353153693e-5, -8.010193625184903e-4, 5.188327685732524e-3, -2.685381193529856e-2, 1.128358514861418e-1, -3.761262582423300e-1, 1.128379165726710)
ERFC_MID = (2.326819970068386e-2, -1.387039388740657e-1, 3.687424674597105e-1, -5.824733027278666e-1, 6.210004621745983e-1, -4.944515323274145e-1, 3.404879937665872e-1, -2.741127028184656e-1, 5.638259427386472e-1)
ERFC_FAR = (-1.047766399936249e1, 1.297719955372516e1, -7.495518717768503, 2.921019019210786, -1.015265279202700, 4.218463358204948e-1, -2.820767439740514e-1, 5.641895067754075e-1)
ATAN = (8.05374449538e-2, -1.38776856032e-1, 1.99777106478e-1, -3.33329491539e-1)


def poly(value, coefs):
    total = jnp.full_like(value, coefs[0])
    for coef in coefs[1:]:
        total = total * value + coef
    return total


def erfc(value):
    square = value * value
    inner = 1.0 - value * poly(square, ERF)
    safe = jnp.maximum(value, 0.5)
    recip = 1.0 / safe
    back = recip * recip
    outer = jnp.exp(-square) * recip * jnp.where(value < 2.0, poly(back, ERFC_MID), poly(back, ERFC_FAR))
    return jnp.where(value < 1.0, inner, outer)


def arctan(value):
    size = jnp.abs(value)
    big, mid = size > 2.414213562373095, size > 0.4142135623730950
    inner = jnp.where(big, -1.0 / jnp.maximum(size, 1.0), jnp.where(mid, (size - 1.0) / (size + 1.0), size))
    base = jnp.where(big, 0.5 * math.pi, jnp.where(mid, 0.25 * math.pi, 0.0))
    square = inner * inner
    result = base + (poly(square, ATAN) * square * inner + inner)
    return jnp.where(value < 0.0, -result, result)


def steps_of(values):
    largest = jnp.max(jnp.abs(values), axis=0, keepdims=True)
    scaled = values * (32767.0 / jnp.maximum(largest, 1e-30))
    return jnp.floor(scaled + 0.5).astype(jnp.int32).astype(jnp.int16), largest * (1.0 / 32767.0)


def two_rows(first, second):
    row = iota((8, first.shape[1]), 0)
    return jnp.where(row == 0, first, jnp.where(row == 1, second, 0.0))


def diagonal(mat):
    on_diag = iota(mat.shape, 0) == iota(mat.shape, 1)
    return jnp.sum(jnp.where(on_diag, mat, 0.0), axis=1, keepdims=True)


def cauchy_terms(zscore):
    angle = 0.5 * math.pi * erfc(jnp.abs(zscore) * (1.0 / math.sqrt(2.0)))
    square = angle * angle
    sign = jnp.where(zscore > 0.0, 1.0, jnp.where(zscore < 0.0, -1.0, 0.0))
    return sign * poly(square, COS) / (angle * poly(square, SIN))


def iota(shape, dim):
    return lax.broadcasted_iota(jnp.int32, shape, dim)


def sweep(pivot, mat):
    shape = mat.shape
    on_row = iota(shape, 0) == pivot
    on_col = iota(shape, 1) == pivot
    row = jnp.sum(jnp.where(on_row, mat, 0.0), axis=0, keepdims=True)
    col = jnp.sum(jnp.where(on_col, mat, 0.0), axis=1, keepdims=True)
    here = iota((shape[0], 1), 0) == pivot
    value = jnp.sum(jnp.where(here, col, 0.0), axis=0, keepdims=True)
    row = jnp.where(iota((1, shape[1]), 1) == pivot, 1.0, row) * (1.0 / value)
    col = jnp.where(here, 0.0, col)
    return jnp.where(on_row, row, jnp.where(on_col, 0.0, mat) - col * row)


def correlate(
    donors, groups, total_blocks, ct_ref, et_ref, place_ref, start_ref, count_ref, x_ref, member_ref, gene_ref, path_ref,
    members_ref, xv, ct, ccc, small, inv_ref, cross_out, sides_out, cross_in, sides_in, beta, beta_sides, slab, expr_t, expr_sums, pieces, wide,
    slot_out, slot_in, near, far,
    x_sem, small_sent, small_got, cross_sent, cross_got, sides_sent, sides_got, beta_sent, beta_got, scale_sent, scale_got, expr_sent, expr_got, slot_sent, slot_got,
    slab_sent, slab_got, member_sent, member_got, own_sem, near_sent, near_got, far_sent, far_got,
):
    my_donor = lax.axis_index("donor")
    my_var = lax.axis_index("var")
    don_rows = ct_ref.shape[1]
    cols = xv.shape[2]
    tiles = cols // TILE
    chunks = don_rows // TILE
    paths = members_ref.shape[1]
    genes_here = member_ref.shape[0]
    half = slab.shape[2]

    def donor_at(step):
        return lax.rem(my_donor + step, donors)

    def var_at(step):
        return lax.rem(my_var + step, groups)

    def load(turn):
        start = pl.multiple_of(donor_at(1 + turn) * cols, cols)
        return pltpu.make_async_copy(x_ref.at[:, pl.ds(start, cols)], xv.at[turn], x_sem.at[turn])

    for turn in range(donors):
        load(turn).start()

    barrier = pltpu.get_barrier_semaphore()
    for step in range(1, donors):
        pl.semaphore_signal(
            barrier, inc=1, device_id=(donor_at(step), my_var), device_id_type=MESH
        )

    def greet(step, carry):
        pl.semaphore_signal(
            barrier, inc=1, device_id=(my_donor, var_at(step)), device_id_type=MESH
        )
        return carry

    lax.fori_loop(1, groups, greet, 0)
    my_core = lax.rem(my_var, 2)
    my_chip = lax.div(my_var, 2)
    for step in range(1, donors):
        pl.semaphore_signal(
            barrier,
            inc=1,
            device_id=(donor_at(step), my_chip * 2 + 1 - my_core),
            device_id_type=MESH,
        )

    thrice = (iota((K, 256), 0) == lax.rem(iota((K, 256), 1), K)).astype(jnp.bfloat16)
    ct[0:K, :] = ct_ref[...]
    own = et_ref[...].astype(jnp.float32)
    ct[K:128, :] = jnp.concatenate(
        [own, jnp.zeros((128 - K - own.shape[0], don_rows), jnp.float32)], axis=0
    ).astype(jnp.bfloat16)
    small[my_donor] = lax.dot_general(
        ct[0:K, :], ct[...], (((1,), (1,)), ((), ())), preferred_element_type=jnp.float32
    )

    def prepare(chunk, carry):
        rows = pl.ds(pl.multiple_of(chunk * 512, 512), 512)
        ccc[rows, :] = lax.dot_general(
            ct[0:K, rows], thrice, (((0,), (0,)), ((), ())), preferred_element_type=jnp.float32
        ).astype(jnp.bfloat16)
        return carry

    lax.fori_loop(0, don_rows // 512, prepare, 0)
    slab[my_var] = jnp.concatenate([own[:, 0:half], own[:, half:]], axis=0).astype(jnp.bfloat16)

    def to_donor(step, src, dst, sent, got):
        return pltpu.make_async_remote_copy(
            src_ref=src,
            dst_ref=dst.at[my_donor],
            send_sem=sent.at[step],
            recv_sem=got.at[my_donor],
            device_id=(donor_at(step), my_var),
            device_id_type=MESH,
        )

    def from_donor(step, dst, sent, got):
        peer = donor_at(step)
        return pltpu.make_async_remote_copy(
            src_ref=dst.at[peer],
            dst_ref=dst.at[peer],
            send_sem=sent.at[step],
            recv_sem=got.at[peer],
            device_id=(peer, my_var),
            device_id_type=MESH,
        )


    def slab_copy(step):
        peer = var_at(step)
        return pltpu.make_async_remote_copy(
            src_ref=slab.at[my_var],
            dst_ref=slab.at[my_var],
            send_sem=slab_sent.at[step],
            recv_sem=slab_got.at[my_var],
            device_id=(my_donor, peer),
            device_id_type=MESH,
        )

    def slab_back(step):
        peer = var_at(step)
        return pltpu.make_async_remote_copy(
            src_ref=slab.at[peer],
            dst_ref=slab.at[peer],
            send_sem=slab_sent.at[step],
            recv_sem=slab_got.at[peer],
            device_id=(my_donor, peer),
            device_id_type=MESH,
        )

    def member_copy(step):
        peer = var_at(step)
        return pltpu.make_async_remote_copy(
            src_ref=member_ref.at[:, pl.ds(pl.multiple_of(peer * paths, 128), paths)],
            dst_ref=members_ref.at[pl.ds(pl.multiple_of(my_var * genes_here, 8), genes_here), :],
            send_sem=member_sent.at[step],
            recv_sem=member_got.at[my_var],
            device_id=(my_donor, peer),
            device_id_type=MESH,
        )

    def member_back(step):
        peer = var_at(step)
        rows = members_ref.at[pl.ds(pl.multiple_of(peer * genes_here, 8), genes_here), :]
        return pltpu.make_async_remote_copy(
            src_ref=rows,
            dst_ref=rows,
            send_sem=member_sent.at[step],
            recv_sem=member_got.at[peer],
            device_id=(my_donor, peer),
            device_id_type=MESH,
        )

    def each(first, last, act):
        def body(step, carry):
            act(step)
            return carry

        lax.fori_loop(first, last, body, 0)

    wide[...] = jnp.zeros_like(wide)
    shrink = lax.rsqrt(jnp.maximum(diagonal(small[my_donor]), 1e-30))

    sweeps = K // (2 * tiles)

    def moments(turn, mat):
        def body(tile, carry):
            if turn >= 2:
                for extra in range(sweeps):
                    carry = sweep(((turn - 2) * tiles + tile) * sweeps + extra, carry)
            lanes = pl.ds(pl.multiple_of(tile * TILE, TILE), TILE)
            product = jnp.dot(
                ct[0:K, :], xv[turn, :, lanes], preferred_element_type=jnp.float32
            )
            square = jnp.zeros((8, TILE), jnp.float32)
            for chunk in range(chunks):
                part = xv[turn, chunk * TILE : (chunk + 1) * TILE, lanes].astype(jnp.float32)
                square = square + jnp.sum((part * part).reshape(TILE // 8, 8, TILE), axis=0)
            rounded, step = steps_of(product * shrink)
            cross_out[turn, :, lanes] = rounded
            sides_out[turn, :, lanes] = two_rows(jnp.sum(square, axis=0, keepdims=True), step)
            return carry

        return lax.fori_loop(0, tiles, body, mat)

    mat = jnp.zeros((K, 128), jnp.float32)
    def send_cross(turn):
        step = turn + 1
        return (
            to_donor(step, cross_out.at[turn], cross_in, cross_sent, cross_got),
            to_donor(step, sides_out.at[turn], sides_in, sides_sent, sides_got),
        )

    for turn in range(donors):
        if turn == 2:
            for step in range(1, donors):
                from_donor(step, small, small_sent, small_got).wait_recv()
            for donor in range(donors):
                mat = mat + small[donor]
            mat = jnp.where(iota((K, 128), 1) < K, mat, 0.0)
            spread = jnp.maximum(diagonal(mat), 1e-30)
        load(turn).wait()
        mat = moments(turn, mat)
        if turn == 0:
            pl.semaphore_wait(barrier, 2 * donors + groups - 3)
            for step in range(1, donors):
                to_donor(step, small.at[my_donor], small, small_sent, small_got).start()
        if turn < donors - 1:
            for copy in send_cross(turn):
                copy.start()
        else:
            cross_in[my_donor] = cross_out[turn]
            sides_in[my_donor] = sides_out[turn]
        if turn == 0:
            each(1, groups, lambda step: slab_copy(step).start())
    inv_ref[...] = mat
    inverse = inv_ref[:, 0:K]

    each(1, groups, lambda step: member_copy(step).start())
    own_member = pltpu.make_async_copy(
        member_ref.at[:, pl.ds(pl.multiple_of(my_var * paths, 128), paths)],
        members_ref.at[pl.ds(pl.multiple_of(my_var * genes_here, 8), genes_here), :],
        own_sem,
    )
    own_member.start()


    for step in range(1, donors):
        from_donor(step, cross_in, cross_sent, cross_got).wait_recv()
        from_donor(step, sides_in, sides_sent, sides_got).wait_recv()
    sizes = [jnp.sqrt(jnp.maximum(diagonal(small[donor]), 1e-30)) for donor in range(donors)]
    widen, narrow = jnp.sqrt(spread), lax.rsqrt(spread)

    def solve(tile, carry):
        lanes = pl.ds(pl.multiple_of(tile * TILE, TILE), TILE)
        cross = jnp.zeros((K, TILE), jnp.float32)
        square = jnp.zeros((1, TILE), jnp.float32)
        for donor in range(donors):
            part = cross_in[donor, :, lanes].astype(jnp.int32).astype(jnp.float32)
            cross = cross + part * sides_in[donor, 1:2, lanes] * sizes[donor]
            square = square + sides_in[donor, 0:1, lanes]
        coef = jnp.dot(
            inverse, cross, precision=HIGHEST, preferred_element_type=jnp.float32
        )
        left = square - jnp.sum(cross * coef, axis=0, keepdims=True)
        scale = lax.rsqrt(jnp.maximum(left, 0.0) + EPSILON)
        rounded, step = steps_of(coef * scale * widen)
        beta[my_donor, :, lanes] = rounded
        beta_sides[my_donor, :, lanes] = two_rows(scale, step)
        return carry

    lax.fori_loop(0, tiles, solve, 0)

    def send_beta(step):
        return (
            to_donor(step, beta.at[my_donor], beta, beta_sent, beta_got),
            to_donor(step, beta_sides.at[my_donor], beta_sides, scale_sent, scale_got),
        )

    for step in range(1, donors):
        for copy in send_beta(step):
            copy.start()

    each(1, groups, lambda step: slab_back(step).wait_recv())
    per_copy = 4

    def unfold(index, carry):
        first = pl.multiple_of(index * per_copy, per_copy)
        part = slab[pl.ds(first, per_copy)].astype(jnp.float32)
        rows = pl.ds(pl.multiple_of(first * 8, per_copy * 8), per_copy * 8)
        expr_t[rows, 0:half] = part[:, 0:8, :].reshape(per_copy * 8, half).astype(jnp.bfloat16)
        expr_t[rows, half : 2 * half] = (
            part[:, 8:16, :].reshape(per_copy * 8, half).astype(jnp.bfloat16)
        )
        return carry

    lax.fori_loop(0, groups // per_copy, unfold, 0)

    genes_all = expr_t.shape[0]
    expr_sums[my_donor, 0:K, :] = lax.dot_general(
        ct[0:K, :], expr_t[...], (((1,), (1,)), ((), ())), preferred_element_type=jnp.float32
    )
    square = jnp.zeros((genes_all, 128), jnp.float32)
    for first in range(0, don_rows, 128):
        part = expr_t[:, first : first + 128].astype(jnp.float32)
        square = square + part * part
    expr_sums[my_donor, K:ROWS, :] = lax.dot_general(
        jnp.ones((ROWS - K, 128), jnp.float32),
        square,
        (((1,), (1,)), ((), ())),
        precision=HIGHEST,
        preferred_element_type=jnp.float32,
    )
    for step in range(1, donors):
        to_donor(step, expr_sums.at[my_donor], expr_sums, expr_sent, expr_got).start()

    def turn_of(step):
        return (step + donors - 1) % donors

    def standardize(step, tile):
        owner, turn = donor_at(step), turn_of(step)
        lanes = pl.ds(pl.multiple_of(tile * TILE, TILE), TILE)
        coef = beta[owner, :, lanes].astype(jnp.int32).astype(jnp.float32)
        coef = coef * beta_sides[owner, 1:2, lanes] * narrow
        scale = beta_sides[owner, 0:1, lanes]
        for piece in range(3):
            rounded = coef.astype(jnp.bfloat16)
            pieces[piece * K : (piece + 1) * K, :] = rounded
            coef = coef - rounded.astype(jnp.float32)
        for first in range(0, don_rows, STRIP):
            rows = slice(first, first + STRIP)
            fitted = jnp.dot(ccc[rows, 0 : 3 * K], pieces[...], preferred_element_type=jnp.float32)
            part = xv[turn, rows, lanes].astype(jnp.float32)
            xv[turn, rows, lanes] = (part * scale - fitted).astype(jnp.bfloat16)

    def pick(step, tile):
        owner, turn = donor_at(step), turn_of(step)
        lanes = pl.ds(pl.multiple_of(tile * TILE, TILE), TILE)
        found = jnp.dot(expr_t[...], xv[turn, :, lanes], preferred_element_type=jnp.float32)
        for side in range(TILE // VB):
            wide[side, PAD : PAD + genes_all, :] = found[:, side * VB : (side + 1) * VB]
        for side in range(TILE // VB):
            block = tile * (TILE // VB) + side
            place = place_ref[owner * (cols // VB) + block]
            base = jnp.right_shift(place - LEAD, 2) + PAD
            found = wide[side, pl.ds(base, 16), :]
            if step:
                slot_out[step, block] = found
            else:
                slot_in[my_donor, block] = found

    each(0, tiles, lambda tile: standardize(0, tile))

    for step in range(1, donors):
        from_donor(step, expr_sums, expr_sent, expr_got).wait_recv()
    sums = expr_sums[0]
    for donor in range(1, donors):
        sums = sums + expr_sums[donor]
    sums = jnp.concatenate([sums, jnp.zeros((128 - ROWS, genes_all), jnp.float32)], axis=0)
    sums = jnp.transpose(sums)
    expr_coef = jnp.dot(
        sums[:, 0:K], inv_ref[...], precision=HIGHEST, preferred_element_type=jnp.float32
    )
    in_cov = iota((genes_all, 128), 1) < K
    expr_ss = sums[:, K : K + 1] - jnp.sum(
        jnp.where(in_cov, sums * expr_coef, 0.0), axis=1, keepdims=True
    )
    expr_scale = lax.rsqrt(jnp.maximum(expr_ss, 0.0) + EPSILON)
    expr_pieces = []
    for piece in range(3):
        rounded = expr_coef.astype(jnp.bfloat16)
        expr_pieces.append(rounded)
        expr_coef = expr_coef - rounded.astype(jnp.float32)
    for first in range(0, don_rows, STRIP):
        lanes = slice(first, first + STRIP)
        resid = expr_t[:, lanes].astype(jnp.float32)
        for part in expr_pieces:
            resid = resid - jnp.dot(part, ct[:, lanes], preferred_element_type=jnp.float32)
        expr_t[:, lanes] = (resid * expr_scale).astype(jnp.bfloat16)

    each(0, tiles, lambda tile: pick(0, tile))
    for step in (1, 3, 2):
        from_donor(step, beta, beta_sent, beta_got).wait_recv()
        from_donor(step, beta_sides, scale_sent, scale_got).wait_recv()

        def both(tile, step=step):
            standardize(step, tile)
            pick(step, tile)

        each(0, tiles, both)
        to_donor(step, slot_out.at[step], slot_in, slot_sent, slot_got).start()

    for step in range(1, donors):
        from_donor(step, slot_in, slot_sent, slot_got).wait_recv()
    donors_all = don_rows * donors
    starts, counts = start_ref[...], count_ref[...]
    gene_row = iota((16, genes_all), 1)
    slot_row = iota((16, genes_all), 0)
    gene_part = jnp.zeros((1, genes_all), jnp.float32)
    for block in range(slot_in.shape[1]):
        total = slot_in[0, block]
        for donor in range(1, donors):
            total = total + slot_in[donor, block]
        terms = jnp.sum(
            cauchy_terms(total * math.sqrt(donors_all - K - 2)), axis=1, keepdims=True
        )
        place = place_ref[my_donor * slot_in.shape[1] + block]
        base = jnp.right_shift(place - LEAD, 2)
        live = (starts <= place) & (place < starts + counts)
        here = (gene_row == slot_row + base) & (slot_row < GMAX)
        column = jnp.sum(jnp.where(here, terms, 0.0), axis=0, keepdims=True)
        gene_part = gene_part + jnp.where(live, column, 0.0)

    near_count, far_count = donors * 2, groups // 2
    my_near = my_donor * 2 + my_core

    def near_id(step):
        place = lax.rem(my_near + step, near_count)
        return place, (lax.div(place, 2), my_chip * 2 + lax.rem(place, 2))

    def far_id(step):
        place = lax.rem(my_chip + step, far_count)
        return place, (my_donor, place * 2 + my_core)

    tail = []
    for buffer, mine, count, where, sent, got in (
        (near, my_near, near_count, near_id, near_sent, near_got),
        (far, my_chip, far_count, far_id, far_sent, far_got),
    ):
        buffer[mine] = gene_part
        for step in range(1, count):
            copy = pltpu.make_async_remote_copy(
                src_ref=buffer.at[mine],
                dst_ref=buffer.at[mine],
                send_sem=sent.at[step],
                recv_sem=got.at[mine],
                device_id=where(step)[1],
                device_id_type=MESH,
            )
            copy.start()
            tail.append(copy)
        for step in range(1, count):
            peer, device = where(step)
            pltpu.make_async_remote_copy(
                src_ref=buffer.at[peer],
                dst_ref=buffer.at[peer],
                send_sem=sent.at[step],
                recv_sem=got.at[peer],
                device_id=device,
                device_id_type=MESH,
            ).wait_recv()
        gene_part = buffer[0]
        for index in range(1, count):
            gene_part = gene_part + buffer[index]

    covered = jnp.minimum(starts + counts, total_blocks) - jnp.maximum(starts, 0)
    gene_stat = gene_part / (VB * covered).astype(jnp.float32)
    gene_value = 0.5 - arctan(gene_stat) / math.pi
    own_gene = iota((genes_here, genes_all), 1) == iota((genes_here, genes_all), 0) + my_var * genes_here
    gene_ref[...] = jnp.broadcast_to(
        jnp.sum(jnp.where(own_gene, gene_value, 0.0), axis=1, keepdims=True), gene_ref.shape
    )
    own_member.wait()
    each(1, groups, lambda step: member_back(step).wait_recv())
    members = members_ref[...]
    path_sum = jnp.dot(
        jnp.broadcast_to(gene_stat, (8, genes_all)),
        members,
        precision=HIGHEST,
        preferred_element_type=jnp.float32,
    )
    path_weight = jnp.sum(members, axis=0, keepdims=True)
    path_ref[...] = (
        0.5 - arctan(path_sum[0:1, :] / jnp.maximum(path_weight, 1.0)) / math.pi
    )
    each(1, groups, lambda step: member_copy(step).wait_send())
    each(1, groups, lambda step: slab_copy(step).wait_send())
    for step in range(1, donors):
        to_donor(step, small.at[my_donor], small, small_sent, small_got).wait_send()
        for copy in (*send_cross(step - 1), *send_beta(step)):
            copy.wait_send()
        to_donor(step, expr_sums.at[my_donor], expr_sums, expr_sent, expr_got).wait_send()
        to_donor(step, slot_out.at[step], slot_in, slot_sent, slot_got).wait_send()
    for copy in tail:
        copy.wait_send()


def local(genotype, block_place, expression, covariates, gene_start, gene_count, membership):
    don_rows, var_cols = genotype.shape
    blocks_here = block_place.shape[0]
    genes_all = gene_start.shape[0]
    genes_here = expression.shape[1]
    groups = lax.axis_size("var")
    donors = lax.axis_size("donor")
    total_blocks = blocks_here * groups
    paths_here = membership.shape[1] // groups
    cols = var_cols // donors
    blocks_own = blocks_here // donors

    vmem = pl.BlockSpec(memory_space=pltpu.VMEM)
    anywhere = pl.BlockSpec(memory_space=pl.ANY)
    dma = pltpu.SemaphoreType.DMA

    def body(*refs):
        correlate(donors, groups, total_blocks, *refs)

    gene_value, path_value = pl.pallas_call(
        body,
        out_shape=(
            jax.ShapeDtypeStruct((genes_here, 128), jnp.float32),
            jax.ShapeDtypeStruct((1, paths_here), jnp.float32),
        ),
        in_specs=[vmem, vmem, pl.BlockSpec(memory_space=pltpu.SMEM), vmem, vmem, anywhere, anywhere],
        out_specs=(vmem, vmem),
        scratch_shapes=[
            pltpu.VMEM((genes_all, paths_here), jnp.float32),
            pltpu.VMEM((donors, don_rows, cols), jnp.bfloat16),
            pltpu.VMEM((128, don_rows), jnp.bfloat16),
            pltpu.VMEM((don_rows, 256), jnp.bfloat16),
            pltpu.VMEM((donors, K, 128), jnp.float32),
            pltpu.VMEM((K, 128), jnp.float32),
            pltpu.VMEM((donors, K, cols), jnp.int16),
            pltpu.VMEM((donors, 8, cols), jnp.float32),
            pltpu.VMEM((donors, K, cols), jnp.int16),
            pltpu.VMEM((donors, 8, cols), jnp.float32),
            pltpu.VMEM((donors, K, cols), jnp.int16),
            pltpu.VMEM((donors, 8, cols), jnp.float32),
            pltpu.VMEM((groups, 16, don_rows // 2), jnp.bfloat16),
            pltpu.VMEM((genes_all, don_rows), jnp.bfloat16),
            pltpu.VMEM((donors, ROWS, genes_all), jnp.float32),
            pltpu.VMEM((3 * K, TILE), jnp.bfloat16),
            pltpu.VMEM((TILE // VB, genes_all + 24, VB), jnp.float32),
            pltpu.VMEM((donors, blocks_own, 16, VB), jnp.float32),
            pltpu.VMEM((donors, blocks_own, 16, VB), jnp.float32),
            pltpu.VMEM((donors * 2, 1, genes_all), jnp.float32),
            pltpu.VMEM((groups // 2, 1, genes_all), jnp.float32),
            *[dma((donors,)) for _ in range(15)],
            *[dma((groups,)) for _ in range(4)],
            dma,
            *[dma((donors * 2,)) for _ in range(2)],
            *[dma((groups // 2,)) for _ in range(2)],
        ],
        compiler_params=pltpu.CompilerParams(
            collective_id=0, has_side_effects=True, vmem_limit_bytes=56 * 2**20
        ),
        name="correlate",
    )(
        covariates.T,
        expression.T,
        block_place,
        gene_start.reshape(1, genes_all),
        gene_count.reshape(1, genes_all),
        genotype,
        membership,
    )

    return (gene_value[:, 0], path_value[0])


def solution(mesh):
    placed = (
        P("donor", "var"),
        P("var"),
        P("donor", "var"),
        P("donor", None),
        P(),
        P(),
        P("var", None),
    )
    return jax.shard_map(
        local, mesh=mesh, in_specs=placed, out_specs=(P("var"), P("var")), check_vma=False
    )
```

```python
import math

import jax
import jax.numpy as jnp
from jax import lax
from jax.experimental import pallas as pl
from jax.experimental.pallas import tpu as pltpu
from jax.sharding import PartitionSpec as P

BPG = 4
CMAX = 52
K = 64
GMAX = 14
VB = 128
EPSILON = 1e-06
HIGHEST = lax.Precision.HIGHEST
MESH = pl.DeviceIdType.MESH
LEAD = CMAX - CMAX // 2 - 1
PAD = 8
ROWS = 72
TILE = 256
STRIP = 512


SIN = (1.6059043837e-10, -2.5052108385e-8, 2.7557319224e-6, -1.9841269841e-4, 8.3333333333e-3, -1.6666666667e-1, 1.0)
COS = (-1.1470745598e-11, 2.0876756988e-9, -2.7557319224e-7, 2.4801587302e-5, -1.3888888889e-3, 4.1666666667e-2, -0.5, 1.0)
ERF = (7.853861353153693e-5, -8.010193625184903e-4, 5.188327685732524e-3, -2.685381193529856e-2, 1.128358514861418e-1, -3.761262582423300e-1, 1.128379165726710)
ERFC_MID = (2.326819970068386e-2, -1.387039388740657e-1, 3.687424674597105e-1, -5.824733027278666e-1, 6.210004621745983e-1, -4.944515323274145e-1, 3.404879937665872e-1, -2.741127028184656e-1, 5.638259427386472e-1)
ERFC_FAR = (-1.047766399936249e1, 1.297719955372516e1, -7.495518717768503, 2.921019019210786, -1.015265279202700, 4.218463358204948e-1, -2.820767439740514e-1, 5.641895067754075e-1)
ATAN = (8.05374449538e-2, -1.38776856032e-1, 1.99777106478e-1, -3.33329491539e-1)


def poly(value, coefs):
    total = jnp.full_like(value, coefs[0])
    for coef in coefs[1:]:
        total = total * value + coef
    return total


def erfc(value):
    square = value * value
    inner = 1.0 - value * poly(square, ERF)
    safe = jnp.maximum(value, 0.5)
    recip = 1.0 / safe
    back = recip * recip
    outer = jnp.exp(-square) * recip * jnp.where(value < 2.0, poly(back, ERFC_MID), poly(back, ERFC_FAR))
    return jnp.where(value < 1.0, inner, outer)


def arctan(value):
    size = jnp.abs(value)
    big, mid = size > 2.414213562373095, size > 0.4142135623730950
    inner = jnp.where(big, -1.0 / jnp.maximum(size, 1.0), jnp.where(mid, (size - 1.0) / (size + 1.0), size))
    base = jnp.where(big, 0.5 * math.pi, jnp.where(mid, 0.25 * math.pi, 0.0))
    square = inner * inner
    result = base + (poly(square, ATAN) * square * inner + inner)
    return jnp.where(value < 0.0, -result, result)


def steps_of(values):
    largest = jnp.max(jnp.abs(values), axis=0, keepdims=True)
    scaled = values * (32767.0 / jnp.maximum(largest, 1e-30))
    return jnp.floor(scaled + 0.5).astype(jnp.int32).astype(jnp.int16), largest * (1.0 / 32767.0)


def two_rows(first, second):
    row = iota((8, first.shape[1]), 0)
    return jnp.where(row == 0, first, jnp.where(row == 1, second, 0.0))


def diagonal(mat):
    on_diag = iota(mat.shape, 0) == iota(mat.shape, 1)
    return jnp.sum(jnp.where(on_diag, mat, 0.0), axis=1, keepdims=True)


def cauchy_terms(zscore):
    angle = 0.5 * math.pi * erfc(jnp.abs(zscore) * (1.0 / math.sqrt(2.0)))
    square = angle * angle
    sign = jnp.where(zscore > 0.0, 1.0, jnp.where(zscore < 0.0, -1.0, 0.0))
    return sign * poly(square, COS) / (angle * poly(square, SIN))


def iota(shape, dim):
    return lax.broadcasted_iota(jnp.int32, shape, dim)


def sweep(pivot, mat):
    shape = mat.shape
    on_row = iota(shape, 0) == pivot
    on_col = iota(shape, 1) == pivot
    row = jnp.sum(jnp.where(on_row, mat, 0.0), axis=0, keepdims=True)
    col = jnp.sum(jnp.where(on_col, mat, 0.0), axis=1, keepdims=True)
    here = iota((shape[0], 1), 0) == pivot
    value = jnp.sum(jnp.where(here, col, 0.0), axis=0, keepdims=True)
    row = jnp.where(iota((1, shape[1]), 1) == pivot, 1.0, row) * (1.0 / value)
    col = jnp.where(here, 0.0, col)
    return jnp.where(on_row, row, jnp.where(on_col, 0.0, mat) - col * row)


def correlate(
    donors, groups, total_blocks, ct_ref, et_ref, place_ref, start_ref, count_ref, x_ref, member_ref, gene_ref, path_ref,
    members_ref, xv, ct, ccc, small, inv_ref, cross_out, sides_out, cross_in, sides_in, beta, beta_sides, slab, expr_t, expr_sums, pieces, wide,
    slot_out, slot_in, near, far,
    x_sem, small_sent, small_got, cross_sent, cross_got, sides_sent, sides_got, beta_sent, beta_got, scale_sent, scale_got, slot_sent, slot_got,
    slab_sent, slab_got, expr_sent, expr_got, member_sent, member_got, own_sem, near_sent, near_got, far_sent, far_got,
):
    my_donor = lax.axis_index("donor")
    my_var = lax.axis_index("var")
    don_rows = ct_ref.shape[1]
    cols = xv.shape[2]
    tiles = cols // TILE
    chunks = don_rows // TILE
    paths = members_ref.shape[1]
    genes_here = member_ref.shape[0]
    half = slab.shape[2]

    def donor_at(step):
        return lax.rem(my_donor + step, donors)

    def var_at(step):
        return lax.rem(my_var + step, groups)

    def load(turn):
        start = pl.multiple_of(donor_at(1 + turn) * cols, cols)
        return pltpu.make_async_copy(x_ref.at[:, pl.ds(start, cols)], xv.at[turn], x_sem.at[turn])

    for turn in range(donors):
        load(turn).start()

    barrier = pltpu.get_barrier_semaphore()
    for step in range(1, donors):
        pl.semaphore_signal(
            barrier, inc=1, device_id=(donor_at(step), my_var), device_id_type=MESH
        )

    def greet(step, carry):
        pl.semaphore_signal(
            barrier, inc=1, device_id=(my_donor, var_at(step)), device_id_type=MESH
        )
        return carry

    lax.fori_loop(1, groups, greet, 0)
    my_core = lax.rem(my_var, 2)
    my_chip = lax.div(my_var, 2)
    for step in range(1, donors):
        pl.semaphore_signal(
            barrier,
            inc=1,
            device_id=(donor_at(step), my_chip * 2 + 1 - my_core),
            device_id_type=MESH,
        )

    thrice = (iota((K, 256), 0) == lax.rem(iota((K, 256), 1), K)).astype(jnp.bfloat16)
    ct[0:K, :] = ct_ref[...]
    own = et_ref[...].astype(jnp.float32)
    ct[K:128, :] = jnp.concatenate(
        [own, jnp.zeros((128 - K - own.shape[0], don_rows), jnp.float32)], axis=0
    ).astype(jnp.bfloat16)
    small[my_donor] = lax.dot_general(
        ct[...], ct[...], (((1,), (1,)), ((), ())), preferred_element_type=jnp.float32
    )[0:ROWS, :]

    def prepare(chunk, carry):
        rows = pl.ds(pl.multiple_of(chunk * 512, 512), 512)
        ccc[rows, :] = lax.dot_general(
            ct[0:K, rows], thrice, (((0,), (0,)), ((), ())), preferred_element_type=jnp.float32
        ).astype(jnp.bfloat16)
        return carry

    lax.fori_loop(0, don_rows // 512, prepare, 0)
    slab[my_var] = jnp.concatenate([own[:, 0:half], own[:, half:]], axis=0).astype(jnp.bfloat16)

    def to_donor(step, src, dst, sent, got):
        return pltpu.make_async_remote_copy(
            src_ref=src,
            dst_ref=dst.at[my_donor],
            send_sem=sent.at[step],
            recv_sem=got.at[my_donor],
            device_id=(donor_at(step), my_var),
            device_id_type=MESH,
        )

    def from_donor(step, dst, sent, got):
        peer = donor_at(step)
        return pltpu.make_async_remote_copy(
            src_ref=dst.at[peer],
            dst_ref=dst.at[peer],
            send_sem=sent.at[step],
            recv_sem=got.at[peer],
            device_id=(peer, my_var),
            device_id_type=MESH,
        )


    def slab_copy(step):
        peer = var_at(step)
        return pltpu.make_async_remote_copy(
            src_ref=slab.at[my_var],
            dst_ref=slab.at[my_var],
            send_sem=slab_sent.at[step],
            recv_sem=slab_got.at[my_var],
            device_id=(my_donor, peer),
            device_id_type=MESH,
        )

    def slab_back(step):
        peer = var_at(step)
        return pltpu.make_async_remote_copy(
            src_ref=slab.at[peer],
            dst_ref=slab.at[peer],
            send_sem=slab_sent.at[step],
            recv_sem=slab_got.at[peer],
            device_id=(my_donor, peer),
            device_id_type=MESH,
        )

    def member_copy(step):
        peer = var_at(step)
        return pltpu.make_async_remote_copy(
            src_ref=member_ref.at[:, pl.ds(pl.multiple_of(peer * paths, 128), paths)],
            dst_ref=members_ref.at[pl.ds(pl.multiple_of(my_var * genes_here, 8), genes_here), :],
            send_sem=member_sent.at[step],
            recv_sem=member_got.at[my_var],
            device_id=(my_donor, peer),
            device_id_type=MESH,
        )

    def member_back(step):
        peer = var_at(step)
        rows = members_ref.at[pl.ds(pl.multiple_of(peer * genes_here, 8), genes_here), :]
        return pltpu.make_async_remote_copy(
            src_ref=rows,
            dst_ref=rows,
            send_sem=member_sent.at[step],
            recv_sem=member_got.at[peer],
            device_id=(my_donor, peer),
            device_id_type=MESH,
        )

    def each(first, last, act):
        def body(step, carry):
            act(step)
            return carry

        lax.fori_loop(first, last, body, 0)

    wide[...] = jnp.zeros_like(wide)
    shrink = lax.rsqrt(jnp.maximum(diagonal(small[my_donor, 0:K, :]), 1e-30))

    sweeps = K // (2 * tiles)

    def moments(turn, mat):
        def body(tile, carry):
            if turn >= 2:
                for extra in range(sweeps):
                    carry = sweep(((turn - 2) * tiles + tile) * sweeps + extra, carry)
            lanes = pl.ds(pl.multiple_of(tile * TILE, TILE), TILE)
            product = jnp.dot(
                ct[0:K, :], xv[turn, :, lanes], preferred_element_type=jnp.float32
            )
            square = jnp.zeros((8, TILE), jnp.float32)
            for chunk in range(chunks):
                part = xv[turn, chunk * TILE : (chunk + 1) * TILE, lanes].astype(jnp.float32)
                square = square + jnp.sum((part * part).reshape(TILE // 8, 8, TILE), axis=0)
            rounded, step = steps_of(product * shrink)
            cross_out[turn, :, lanes] = rounded
            sides_out[turn, :, lanes] = two_rows(jnp.sum(square, axis=0, keepdims=True), step)
            return carry

        return lax.fori_loop(0, tiles, body, mat)

    mat = jnp.zeros((K, 128), jnp.float32)
    def send_cross(turn):
        step = turn + 1
        return (
            to_donor(step, cross_out.at[turn], cross_in, cross_sent, cross_got),
            to_donor(step, sides_out.at[turn], sides_in, sides_sent, sides_got),
        )

    for turn in range(donors):
        if turn == 2:
            for step in range(1, donors):
                from_donor(step, small, small_sent, small_got).wait_recv()
            expr_rows = jnp.zeros((ROWS - K, 128), jnp.float32)
            for donor in range(donors):
                mat = mat + small[donor, 0:K, :]
                expr_rows = expr_rows + small[donor, K:ROWS, :]
            mat = jnp.where(iota((K, 128), 1) < K, mat, 0.0)
            spread = jnp.maximum(diagonal(mat), 1e-30)
        load(turn).wait()
        mat = moments(turn, mat)
        if turn == 0:
            pl.semaphore_wait(barrier, 2 * donors + groups - 3)
            for step in range(1, donors):
                to_donor(step, small.at[my_donor], small, small_sent, small_got).start()
        if turn < donors - 1:
            for copy in send_cross(turn):
                copy.start()
        else:
            cross_in[my_donor] = cross_out[turn]
            sides_in[my_donor] = sides_out[turn]
        if turn == 0:
            each(1, groups, lambda step: slab_copy(step).start())
    inv_ref[...] = mat
    inverse = inv_ref[:, 0:K]

    coef_shape = (genes_here, 128)
    expr_coef = jnp.dot(
        expr_rows[:, 0:K], mat, precision=HIGHEST, preferred_element_type=jnp.float32
    )
    on_own = iota(coef_shape, 1) == iota(coef_shape, 0) + K
    expr_sq = jnp.sum(jnp.where(on_own, expr_rows, 0.0), axis=1, keepdims=True)
    in_cov = iota(coef_shape, 1) < K
    expr_ss = expr_sq - jnp.sum(
        jnp.where(in_cov, expr_rows * expr_coef, 0.0), axis=1, keepdims=True
    )
    expr_scale = lax.rsqrt(jnp.maximum(expr_ss, 0.0) + EPSILON)
    expr_sums[my_var] = jnp.where(in_cov, expr_coef, expr_scale)

    def coef_copy(step):
        return pltpu.make_async_remote_copy(
            src_ref=expr_sums.at[my_var],
            dst_ref=expr_sums.at[my_var],
            send_sem=expr_sent.at[step],
            recv_sem=expr_got.at[my_var],
            device_id=(my_donor, var_at(step)),
            device_id_type=MESH,
        )

    def coef_back(step):
        peer = var_at(step)
        return pltpu.make_async_remote_copy(
            src_ref=expr_sums.at[peer],
            dst_ref=expr_sums.at[peer],
            send_sem=expr_sent.at[step],
            recv_sem=expr_got.at[peer],
            device_id=(my_donor, peer),
            device_id_type=MESH,
        )

    each(1, groups, lambda step: coef_copy(step).start())

    each(1, groups, lambda step: member_copy(step).start())
    own_member = pltpu.make_async_copy(
        member_ref.at[:, pl.ds(pl.multiple_of(my_var * paths, 128), paths)],
        members_ref.at[pl.ds(pl.multiple_of(my_var * genes_here, 8), genes_here), :],
        own_sem,
    )
    own_member.start()


    for step in range(1, donors):
        from_donor(step, cross_in, cross_sent, cross_got).wait_recv()
        from_donor(step, sides_in, sides_sent, sides_got).wait_recv()
    sizes = [jnp.sqrt(jnp.maximum(diagonal(small[donor, 0:K, :]), 1e-30)) for donor in range(donors)]
    widen, narrow = jnp.sqrt(spread), lax.rsqrt(spread)

    def solve(tile, carry):
        lanes = pl.ds(pl.multiple_of(tile * TILE, TILE), TILE)
        cross = jnp.zeros((K, TILE), jnp.float32)
        square = jnp.zeros((1, TILE), jnp.float32)
        for donor in range(donors):
            part = cross_in[donor, :, lanes].astype(jnp.int32).astype(jnp.float32)
            cross = cross + part * sides_in[donor, 1:2, lanes] * sizes[donor]
            square = square + sides_in[donor, 0:1, lanes]
        coef = jnp.dot(
            inverse, cross, precision=HIGHEST, preferred_element_type=jnp.float32
        )
        left = square - jnp.sum(cross * coef, axis=0, keepdims=True)
        scale = lax.rsqrt(jnp.maximum(left, 0.0) + EPSILON)
        rounded, step = steps_of(coef * scale * widen)
        beta[my_donor, :, lanes] = rounded
        beta_sides[my_donor, :, lanes] = two_rows(scale, step)
        return carry

    lax.fori_loop(0, tiles, solve, 0)

    def send_beta(step):
        return (
            to_donor(step, beta.at[my_donor], beta, beta_sent, beta_got),
            to_donor(step, beta_sides.at[my_donor], beta_sides, scale_sent, scale_got),
        )

    for step in (1, 3, 2):
        for copy in send_beta(step):
            copy.start()

    genes_all = expr_t.shape[0]

    def turn_of(step):
        return (step + donors - 1) % donors

    def standardize(step, tile):
        owner, turn = donor_at(step), turn_of(step)
        lanes = pl.ds(pl.multiple_of(tile * TILE, TILE), TILE)
        coef = beta[owner, :, lanes].astype(jnp.int32).astype(jnp.float32)
        coef = coef * beta_sides[owner, 1:2, lanes] * narrow
        scale = beta_sides[owner, 0:1, lanes]
        for piece in range(3):
            rounded = coef.astype(jnp.bfloat16)
            pieces[piece * K : (piece + 1) * K, :] = rounded
            coef = coef - rounded.astype(jnp.float32)
        for first in range(0, don_rows, STRIP):
            rows = slice(first, first + STRIP)
            fitted = jnp.dot(ccc[rows, 0 : 3 * K], pieces[...], preferred_element_type=jnp.float32)
            part = xv[turn, rows, lanes].astype(jnp.float32)
            xv[turn, rows, lanes] = (part * scale - fitted).astype(jnp.bfloat16)

    def pick(step, tile):
        owner, turn = donor_at(step), turn_of(step)
        lanes = pl.ds(pl.multiple_of(tile * TILE, TILE), TILE)
        found = jnp.dot(expr_t[...], xv[turn, :, lanes], preferred_element_type=jnp.float32)
        for side in range(TILE // VB):
            wide[side, PAD : PAD + genes_all, :] = found[:, side * VB : (side + 1) * VB]
        for side in range(TILE // VB):
            block = tile * (TILE // VB) + side
            place = place_ref[owner * (cols // VB) + block]
            base = jnp.right_shift(place - LEAD, 2) + PAD
            found = wide[side, pl.ds(base, 16), :]
            if step:
                slot_out[step, block] = found
            else:
                slot_in[my_donor, block] = found

    each(0, tiles, lambda tile: standardize(0, tile))

    each(1, groups, lambda step: slab_back(step).wait_recv())
    per_copy = 4

    def unfold(index, carry):
        first = pl.multiple_of(index * per_copy, per_copy)
        part = slab[pl.ds(first, per_copy)].astype(jnp.float32)
        rows = pl.ds(pl.multiple_of(first * 8, per_copy * 8), per_copy * 8)
        expr_t[rows, 0:half] = part[:, 0:8, :].reshape(per_copy * 8, half).astype(jnp.bfloat16)
        expr_t[rows, half : 2 * half] = (
            part[:, 8:16, :].reshape(per_copy * 8, half).astype(jnp.bfloat16)
        )
        return carry

    lax.fori_loop(0, groups // per_copy, unfold, 0)
    each(1, groups, lambda step: coef_back(step).wait_recv())
    expr_coef = expr_sums[...].reshape(genes_all, 128)
    expr_scale = expr_coef[:, K : K + 1]
    expr_coef = jnp.where(iota((genes_all, 128), 1) < K, expr_coef, 0.0)
    expr_pieces = []
    for piece in range(3):
        rounded = expr_coef.astype(jnp.bfloat16)
        expr_pieces.append(rounded)
        expr_coef = expr_coef - rounded.astype(jnp.float32)
    for first in range(0, don_rows, STRIP):
        lanes = slice(first, first + STRIP)
        resid = expr_t[:, lanes].astype(jnp.float32)
        for part in expr_pieces:
            resid = resid - jnp.dot(part, ct[:, lanes], preferred_element_type=jnp.float32)
        expr_t[:, lanes] = (resid * expr_scale).astype(jnp.bfloat16)

    each(0, tiles, lambda tile: pick(0, tile))
    for step in (1, 3, 2):
        from_donor(step, beta, beta_sent, beta_got).wait_recv()
        from_donor(step, beta_sides, scale_sent, scale_got).wait_recv()

        def both(tile, step=step):
            standardize(step, tile)
            pick(step, tile)

        each(0, tiles, both)
        to_donor(step, slot_out.at[step], slot_in, slot_sent, slot_got).start()

    for step in range(1, donors):
        from_donor(step, slot_in, slot_sent, slot_got).wait_recv()
    donors_all = don_rows * donors
    starts, counts = start_ref[...], count_ref[...]
    gene_row = iota((16, genes_all), 1)
    slot_row = iota((16, genes_all), 0)
    gene_part = jnp.zeros((1, genes_all), jnp.float32)
    for block in range(slot_in.shape[1]):
        total = slot_in[0, block]
        for donor in range(1, donors):
            total = total + slot_in[donor, block]
        terms = jnp.sum(
            cauchy_terms(total * math.sqrt(donors_all - K - 2)), axis=1, keepdims=True
        )
        place = place_ref[my_donor * slot_in.shape[1] + block]
        base = jnp.right_shift(place - LEAD, 2)
        live = (starts <= place) & (place < starts + counts)
        here = (gene_row == slot_row + base) & (slot_row < GMAX)
        column = jnp.sum(jnp.where(here, terms, 0.0), axis=0, keepdims=True)
        gene_part = gene_part + jnp.where(live, column, 0.0)

    near_count, far_count = donors * 2, groups // 2
    my_near = my_donor * 2 + my_core

    def near_id(step):
        place = lax.rem(my_near + step, near_count)
        return place, (lax.div(place, 2), my_chip * 2 + lax.rem(place, 2))

    def far_id(step):
        place = lax.rem(my_chip + step, far_count)
        return place, (my_donor, place * 2 + my_core)

    tail = []
    for buffer, mine, count, where, sent, got in (
        (near, my_near, near_count, near_id, near_sent, near_got),
        (far, my_chip, far_count, far_id, far_sent, far_got),
    ):
        buffer[mine] = gene_part
        for step in range(1, count):
            copy = pltpu.make_async_remote_copy(
                src_ref=buffer.at[mine],
                dst_ref=buffer.at[mine],
                send_sem=sent.at[step],
                recv_sem=got.at[mine],
                device_id=where(step)[1],
                device_id_type=MESH,
            )
            copy.start()
            tail.append(copy)
        for step in range(1, count):
            peer, device = where(step)
            pltpu.make_async_remote_copy(
                src_ref=buffer.at[peer],
                dst_ref=buffer.at[peer],
                send_sem=sent.at[step],
                recv_sem=got.at[peer],
                device_id=device,
                device_id_type=MESH,
            ).wait_recv()
        gene_part = buffer[0]
        for index in range(1, count):
            gene_part = gene_part + buffer[index]

    covered = jnp.minimum(starts + counts, total_blocks) - jnp.maximum(starts, 0)
    gene_stat = gene_part / (VB * covered).astype(jnp.float32)
    gene_value = 0.5 - arctan(gene_stat) / math.pi
    own_gene = iota((genes_here, genes_all), 1) == iota((genes_here, genes_all), 0) + my_var * genes_here
    gene_ref[...] = jnp.broadcast_to(
        jnp.sum(jnp.where(own_gene, gene_value, 0.0), axis=1, keepdims=True), gene_ref.shape
    )
    own_member.wait()
    each(1, groups, lambda step: member_back(step).wait_recv())
    members = members_ref[...]
    path_sum = jnp.dot(
        jnp.broadcast_to(gene_stat, (8, genes_all)),
        members,
        precision=HIGHEST,
        preferred_element_type=jnp.float32,
    )
    path_weight = jnp.sum(members, axis=0, keepdims=True)
    path_ref[...] = (
        0.5 - arctan(path_sum[0:1, :] / jnp.maximum(path_weight, 1.0)) / math.pi
    )
    each(1, groups, lambda step: member_copy(step).wait_send())
    each(1, groups, lambda step: slab_copy(step).wait_send())
    each(1, groups, lambda step: coef_copy(step).wait_send())
    for step in range(1, donors):
        to_donor(step, small.at[my_donor], small, small_sent, small_got).wait_send()
        for copy in (*send_cross(step - 1), *send_beta(step)):
            copy.wait_send()
        to_donor(step, slot_out.at[step], slot_in, slot_sent, slot_got).wait_send()
    for copy in tail:
        copy.wait_send()


def local(genotype, block_place, expression, covariates, gene_start, gene_count, membership):
    don_rows, var_cols = genotype.shape
    blocks_here = block_place.shape[0]
    genes_all = gene_start.shape[0]
    genes_here = expression.shape[1]
    groups = lax.axis_size("var")
    donors = lax.axis_size("donor")
    total_blocks = blocks_here * groups
    paths_here = membership.shape[1] // groups
    cols = var_cols // donors
    blocks_own = blocks_here // donors

    vmem = pl.BlockSpec(memory_space=pltpu.VMEM)
    anywhere = pl.BlockSpec(memory_space=pl.ANY)
    dma = pltpu.SemaphoreType.DMA

    def body(*refs):
        correlate(donors, groups, total_blocks, *refs)

    gene_value, path_value = pl.pallas_call(
        body,
        out_shape=(
            jax.ShapeDtypeStruct((genes_here, 128), jnp.float32),
            jax.ShapeDtypeStruct((1, paths_here), jnp.float32),
        ),
        in_specs=[vmem, vmem, pl.BlockSpec(memory_space=pltpu.SMEM), vmem, vmem, anywhere, anywhere],
        out_specs=(vmem, vmem),
        scratch_shapes=[
            pltpu.VMEM((genes_all, paths_here), jnp.float32),
            pltpu.VMEM((donors, don_rows, cols), jnp.bfloat16),
            pltpu.VMEM((128, don_rows), jnp.bfloat16),
            pltpu.VMEM((don_rows, 256), jnp.bfloat16),
            pltpu.VMEM((donors, ROWS, 128), jnp.float32),
            pltpu.VMEM((K, 128), jnp.float32),
            pltpu.VMEM((donors, K, cols), jnp.int16),
            pltpu.VMEM((donors, 8, cols), jnp.float32),
            pltpu.VMEM((donors, K, cols), jnp.int16),
            pltpu.VMEM((donors, 8, cols), jnp.float32),
            pltpu.VMEM((donors, K, cols), jnp.int16),
            pltpu.VMEM((donors, 8, cols), jnp.float32),
            pltpu.VMEM((groups, 16, don_rows // 2), jnp.bfloat16),
            pltpu.VMEM((genes_all, don_rows), jnp.bfloat16),
            pltpu.VMEM((groups, genes_here, 128), jnp.float32),
            pltpu.VMEM((3 * K, TILE), jnp.bfloat16),
            pltpu.VMEM((TILE // VB, genes_all + 24, VB), jnp.float32),
            pltpu.VMEM((donors, blocks_own, 16, VB), jnp.float32),
            pltpu.VMEM((donors, blocks_own, 16, VB), jnp.float32),
            pltpu.VMEM((donors * 2, 1, genes_all), jnp.float32),
            pltpu.VMEM((groups // 2, 1, genes_all), jnp.float32),
            *[dma((donors,)) for _ in range(13)],
            *[dma((groups,)) for _ in range(6)],
            dma,
            *[dma((donors * 2,)) for _ in range(2)],
            *[dma((groups // 2,)) for _ in range(2)],
        ],
        compiler_params=pltpu.CompilerParams(
            collective_id=0, has_side_effects=True, vmem_limit_bytes=56 * 2**20
        ),
        name="correlate",
    )(
        covariates.T,
        expression.T,
        block_place,
        gene_start.reshape(1, genes_all),
        gene_count.reshape(1, genes_all),
        genotype,
        membership,
    )

    return (gene_value[:, 0], path_value[0])


def solution(mesh):
    placed = (
        P("donor", "var"),
        P("var"),
        P("donor", "var"),
        P("donor", None),
        P(),
        P(),
        P("var", None),
    )
    return jax.shard_map(
        local, mesh=mesh, in_specs=placed, out_specs=(P("var"), P("var")), check_vma=False
    )
```

```python
import math

import jax
import jax.numpy as jnp
from jax import lax
from jax.experimental import pallas as pl
from jax.experimental.pallas import tpu as pltpu
from jax.sharding import PartitionSpec as P

BPG = 4
CMAX = 52
K = 64
GMAX = 14
VB = 128
EPSILON = 1e-06
HIGHEST = lax.Precision.HIGHEST
MESH = pl.DeviceIdType.MESH
LEAD = CMAX - CMAX // 2 - 1
PAD = 8
ROWS = 72
TILE = 256
STRIP = 512


SIN = (1.6059043837e-10, -2.5052108385e-8, 2.7557319224e-6, -1.9841269841e-4, 8.3333333333e-3, -1.6666666667e-1, 1.0)
COS = (-1.1470745598e-11, 2.0876756988e-9, -2.7557319224e-7, 2.4801587302e-5, -1.3888888889e-3, 4.1666666667e-2, -0.5, 1.0)
ERF = (7.853861353153693e-5, -8.010193625184903e-4, 5.188327685732524e-3, -2.685381193529856e-2, 1.128358514861418e-1, -3.761262582423300e-1, 1.128379165726710)
ERFC_MID = (2.326819970068386e-2, -1.387039388740657e-1, 3.687424674597105e-1, -5.824733027278666e-1, 6.210004621745983e-1, -4.944515323274145e-1, 3.404879937665872e-1, -2.741127028184656e-1, 5.638259427386472e-1)
ERFC_FAR = (-1.047766399936249e1, 1.297719955372516e1, -7.495518717768503, 2.921019019210786, -1.015265279202700, 4.218463358204948e-1, -2.820767439740514e-1, 5.641895067754075e-1)
ATAN = (8.05374449538e-2, -1.38776856032e-1, 1.99777106478e-1, -3.33329491539e-1)


def poly(value, coefs):
    total = jnp.full_like(value, coefs[0])
    for coef in coefs[1:]:
        total = total * value + coef
    return total


def erfc(value):
    square = value * value
    inner = 1.0 - value * poly(square, ERF)
    safe = jnp.maximum(value, 0.5)
    recip = 1.0 / safe
    back = recip * recip
    outer = jnp.exp(-square) * recip * jnp.where(value < 2.0, poly(back, ERFC_MID), poly(back, ERFC_FAR))
    return jnp.where(value < 1.0, inner, outer)


def arctan(value):
    size = jnp.abs(value)
    big, mid = size > 2.414213562373095, size > 0.4142135623730950
    inner = jnp.where(big, -1.0 / jnp.maximum(size, 1.0), jnp.where(mid, (size - 1.0) / (size + 1.0), size))
    base = jnp.where(big, 0.5 * math.pi, jnp.where(mid, 0.25 * math.pi, 0.0))
    square = inner * inner
    result = base + (poly(square, ATAN) * square * inner + inner)
    return jnp.where(value < 0.0, -result, result)


def steps_of(values):
    largest = jnp.max(jnp.abs(values), axis=0, keepdims=True)
    scaled = values * (32767.0 / jnp.maximum(largest, 1e-30))
    return jnp.floor(scaled + 0.5).astype(jnp.int32).astype(jnp.int16), largest * (1.0 / 32767.0)


def two_rows(first, second):
    row = iota((8, first.shape[1]), 0)
    return jnp.where(row == 0, first, jnp.where(row == 1, second, 0.0))


def diagonal(mat):
    on_diag = iota(mat.shape, 0) == iota(mat.shape, 1)
    return jnp.sum(jnp.where(on_diag, mat, 0.0), axis=1, keepdims=True)


def cauchy_terms(zscore):
    angle = 0.5 * math.pi * erfc(jnp.abs(zscore) * (1.0 / math.sqrt(2.0)))
    square = angle * angle
    sign = jnp.where(zscore > 0.0, 1.0, jnp.where(zscore < 0.0, -1.0, 0.0))
    return sign * poly(square, COS) / (angle * poly(square, SIN))


def iota(shape, dim):
    return lax.broadcasted_iota(jnp.int32, shape, dim)


def sweep(pivot, mat):
    shape = mat.shape
    on_row = iota(shape, 0) == pivot
    on_col = iota(shape, 1) == pivot
    row = jnp.sum(jnp.where(on_row, mat, 0.0), axis=0, keepdims=True)
    col = jnp.sum(jnp.where(on_col, mat, 0.0), axis=1, keepdims=True)
    here = iota((shape[0], 1), 0) == pivot
    value = jnp.sum(jnp.where(here, col, 0.0), axis=0, keepdims=True)
    row = jnp.where(iota((1, shape[1]), 1) == pivot, 1.0, row) * (1.0 / value)
    col = jnp.where(here, 0.0, col)
    return jnp.where(on_row, row, jnp.where(on_col, 0.0, mat) - col * row)


def correlate(
    donors, groups, total_blocks, ct_ref, et_ref, place_ref, start_ref, count_ref, x_ref, member_ref, gene_ref, path_ref,
    members_ref, xv, ct, ccc, small, inv_ref, cross_out, sides_out, cross_in, sides_in, beta, beta_sides, slab, expr_t, expr_sums, pieces, wide,
    slot_out, slot_in, near, far,
    x_sem, small_sent, small_got, cross_sent, cross_got, sides_sent, sides_got, beta_sent, beta_got, scale_sent, scale_got, slot_sent, slot_got,
    slab_sent, slab_got, expr_sent, expr_got, member_sent, member_got, own_sem, near_sent, near_got, far_sent, far_got,
):
    my_donor = lax.axis_index("donor")
    my_var = lax.axis_index("var")
    don_rows = ct_ref.shape[1]
    cols = xv.shape[2]
    tiles = cols // TILE
    chunks = don_rows // TILE
    paths = members_ref.shape[1]
    genes_here = member_ref.shape[0]
    half = slab.shape[2]

    def donor_at(step):
        return lax.rem(my_donor + step, donors)

    def var_at(step):
        return lax.rem(my_var + step, groups)

    def load(turn):
        start = pl.multiple_of(donor_at(1 + turn) * cols, cols)
        return pltpu.make_async_copy(x_ref.at[:, pl.ds(start, cols)], xv.at[turn], x_sem.at[turn])

    for turn in range(donors):
        load(turn).start()

    barrier = pltpu.get_barrier_semaphore()
    for step in range(1, donors):
        pl.semaphore_signal(
            barrier, inc=1, device_id=(donor_at(step), my_var), device_id_type=MESH
        )

    def greet(step, carry):
        pl.semaphore_signal(
            barrier, inc=1, device_id=(my_donor, var_at(step)), device_id_type=MESH
        )
        return carry

    lax.fori_loop(1, groups, greet, 0)
    my_core = lax.rem(my_var, 2)
    my_chip = lax.div(my_var, 2)
    for step in range(1, donors):
        pl.semaphore_signal(
            barrier,
            inc=1,
            device_id=(donor_at(step), my_chip * 2 + 1 - my_core),
            device_id_type=MESH,
        )

    thrice = (iota((K, 256), 0) == lax.rem(iota((K, 256), 1), K)).astype(jnp.bfloat16)
    ct[0:K, :] = ct_ref[...]
    own = et_ref[...].astype(jnp.float32)
    ct[K:128, :] = jnp.concatenate(
        [own, jnp.zeros((128 - K - own.shape[0], don_rows), jnp.float32)], axis=0
    ).astype(jnp.bfloat16)
    small[my_donor] = lax.dot_general(
        ct[...], ct[...], (((1,), (1,)), ((), ())), preferred_element_type=jnp.float32
    )[0:ROWS, :]

    def prepare(chunk, carry):
        rows = pl.ds(pl.multiple_of(chunk * 512, 512), 512)
        ccc[rows, :] = lax.dot_general(
            ct[0:K, rows], thrice, (((0,), (0,)), ((), ())), preferred_element_type=jnp.float32
        ).astype(jnp.bfloat16)
        return carry

    lax.fori_loop(0, don_rows // 512, prepare, 0)
    slab[my_var] = jnp.concatenate([own[:, 0:half], own[:, half:]], axis=0).astype(jnp.bfloat16)

    def to_donor(step, src, dst, sent, got):
        return pltpu.make_async_remote_copy(
            src_ref=src,
            dst_ref=dst.at[my_donor],
            send_sem=sent.at[step],
            recv_sem=got.at[my_donor],
            device_id=(donor_at(step), my_var),
            device_id_type=MESH,
        )

    def from_donor(step, dst, sent, got):
        peer = donor_at(step)
        return pltpu.make_async_remote_copy(
            src_ref=dst.at[peer],
            dst_ref=dst.at[peer],
            send_sem=sent.at[step],
            recv_sem=got.at[peer],
            device_id=(peer, my_var),
            device_id_type=MESH,
        )


    def slab_copy(step):
        peer = var_at(step)
        return pltpu.make_async_remote_copy(
            src_ref=slab.at[my_var],
            dst_ref=slab.at[my_var],
            send_sem=slab_sent.at[step],
            recv_sem=slab_got.at[my_var],
            device_id=(my_donor, peer),
            device_id_type=MESH,
        )

    def slab_back(step):
        peer = var_at(step)
        return pltpu.make_async_remote_copy(
            src_ref=slab.at[peer],
            dst_ref=slab.at[peer],
            send_sem=slab_sent.at[step],
            recv_sem=slab_got.at[peer],
            device_id=(my_donor, peer),
            device_id_type=MESH,
        )

    def member_copy(step):
        peer = var_at(step)
        return pltpu.make_async_remote_copy(
            src_ref=member_ref.at[:, pl.ds(pl.multiple_of(peer * paths, 128), paths)],
            dst_ref=members_ref.at[pl.ds(pl.multiple_of(my_var * genes_here, 8), genes_here), :],
            send_sem=member_sent.at[step],
            recv_sem=member_got.at[my_var],
            device_id=(my_donor, peer),
            device_id_type=MESH,
        )

    def member_back(step):
        peer = var_at(step)
        rows = members_ref.at[pl.ds(pl.multiple_of(peer * genes_here, 8), genes_here), :]
        return pltpu.make_async_remote_copy(
            src_ref=rows,
            dst_ref=rows,
            send_sem=member_sent.at[step],
            recv_sem=member_got.at[peer],
            device_id=(my_donor, peer),
            device_id_type=MESH,
        )

    def each(first, last, act):
        def body(step, carry):
            act(step)
            return carry

        lax.fori_loop(first, last, body, 0)

    wide[...] = jnp.zeros_like(wide)
    shrink = lax.rsqrt(jnp.maximum(diagonal(small[my_donor, 0:K, :]), 1e-30))

    sweeps = K // (2 * tiles)

    def moments(turn, mat):
        def body(tile, carry):
            if turn >= 2:
                for extra in range(sweeps):
                    carry = sweep(((turn - 2) * tiles + tile) * sweeps + extra, carry)
            lanes = pl.ds(pl.multiple_of(tile * TILE, TILE), TILE)
            product = jnp.dot(
                ct[0:K, :], xv[turn, :, lanes], preferred_element_type=jnp.float32
            )
            square = jnp.zeros((8, TILE), jnp.float32)
            for chunk in range(chunks):
                part = xv[turn, chunk * TILE : (chunk + 1) * TILE, lanes].astype(jnp.float32)
                square = square + jnp.sum((part * part).reshape(TILE // 8, 8, TILE), axis=0)
            rounded, step = steps_of(product * shrink)
            cross_out[turn, :, lanes] = rounded
            sides_out[turn, :, lanes] = two_rows(jnp.sum(square, axis=0, keepdims=True), step)
            return carry

        return lax.fori_loop(0, tiles, body, mat)

    mat = jnp.zeros((K, 128), jnp.float32)
    def send_cross(turn):
        step = turn + 1
        return (
            to_donor(step, cross_out.at[turn], cross_in, cross_sent, cross_got),
            to_donor(step, sides_out.at[turn], sides_in, sides_sent, sides_got),
        )

    for turn in range(donors):
        if turn == 2:
            for step in range(1, donors):
                from_donor(step, small, small_sent, small_got).wait_recv()
            expr_rows = jnp.zeros((ROWS - K, 128), jnp.float32)
            for donor in range(donors):
                mat = mat + small[donor, 0:K, :]
                expr_rows = expr_rows + small[donor, K:ROWS, :]
            mat = jnp.where(iota((K, 128), 1) < K, mat, 0.0)
            spread = jnp.maximum(diagonal(mat), 1e-30)
        load(turn).wait()
        mat = moments(turn, mat)
        if turn == 0:
            pl.semaphore_wait(barrier, 2 * donors + groups - 3)
            for step in range(1, donors):
                to_donor(step, small.at[my_donor], small, small_sent, small_got).start()
        if turn < donors - 1:
            for copy in send_cross(turn):
                copy.start()
        else:
            cross_in[my_donor] = cross_out[turn]
            sides_in[my_donor] = sides_out[turn]
        if turn == 0:
            each(1, groups, lambda step: slab_copy(step).start())
    inv_ref[...] = mat
    inverse = inv_ref[:, 0:K]

    coef_shape = (genes_here, 128)
    expr_coef = jnp.dot(
        expr_rows[:, 0:K], mat, precision=HIGHEST, preferred_element_type=jnp.float32
    )
    on_own = iota(coef_shape, 1) == iota(coef_shape, 0) + K
    expr_sq = jnp.sum(jnp.where(on_own, expr_rows, 0.0), axis=1, keepdims=True)
    in_cov = iota(coef_shape, 1) < K
    expr_ss = expr_sq - jnp.sum(
        jnp.where(in_cov, expr_rows * expr_coef, 0.0), axis=1, keepdims=True
    )
    expr_scale = lax.rsqrt(jnp.maximum(expr_ss, 0.0) + EPSILON)
    expr_sums[my_var] = jnp.where(in_cov, expr_coef, expr_scale)

    def coef_copy(step):
        return pltpu.make_async_remote_copy(
            src_ref=expr_sums.at[my_var],
            dst_ref=expr_sums.at[my_var],
            send_sem=expr_sent.at[step],
            recv_sem=expr_got.at[my_var],
            device_id=(my_donor, var_at(step)),
            device_id_type=MESH,
        )

    def coef_back(step):
        peer = var_at(step)
        return pltpu.make_async_remote_copy(
            src_ref=expr_sums.at[peer],
            dst_ref=expr_sums.at[peer],
            send_sem=expr_sent.at[step],
            recv_sem=expr_got.at[peer],
            device_id=(my_donor, peer),
            device_id_type=MESH,
        )

    each(1, groups, lambda step: coef_copy(step).start())

    each(1, groups, lambda step: member_copy(step).start())
    own_member = pltpu.make_async_copy(
        member_ref.at[:, pl.ds(pl.multiple_of(my_var * paths, 128), paths)],
        members_ref.at[pl.ds(pl.multiple_of(my_var * genes_here, 8), genes_here), :],
        own_sem,
    )
    own_member.start()


    for step in range(1, donors):
        from_donor(step, cross_in, cross_sent, cross_got).wait_recv()
        from_donor(step, sides_in, sides_sent, sides_got).wait_recv()
    sizes = [jnp.sqrt(jnp.maximum(diagonal(small[donor, 0:K, :]), 1e-30)) for donor in range(donors)]
    widen, narrow = jnp.sqrt(spread), lax.rsqrt(spread)

    def solve(tile, carry):
        lanes = pl.ds(pl.multiple_of(tile * TILE, TILE), TILE)
        cross = jnp.zeros((K, TILE), jnp.float32)
        square = jnp.zeros((1, TILE), jnp.float32)
        for donor in range(donors):
            part = cross_in[donor, :, lanes].astype(jnp.int32).astype(jnp.float32)
            cross = cross + part * sides_in[donor, 1:2, lanes] * sizes[donor]
            square = square + sides_in[donor, 0:1, lanes]
        coef = jnp.dot(
            inverse, cross, precision=HIGHEST, preferred_element_type=jnp.float32
        )
        left = square - jnp.sum(cross * coef, axis=0, keepdims=True)
        scale = lax.rsqrt(jnp.maximum(left, 0.0) + EPSILON)
        rounded, step = steps_of(coef * scale * widen)
        beta[my_donor, :, lanes] = rounded
        beta_sides[my_donor, :, lanes] = two_rows(scale, step)
        return carry

    lax.fori_loop(0, tiles, solve, 0)

    def send_beta(step):
        return (
            to_donor(step, beta.at[my_donor], beta, beta_sent, beta_got),
            to_donor(step, beta_sides.at[my_donor], beta_sides, scale_sent, scale_got),
        )

    for step in (1, 3, 2):
        for copy in send_beta(step):
            copy.start()

    genes_all = expr_t.shape[0]

    def turn_of(step):
        return (step + donors - 1) % donors

    def lanes_of(tile):
        if isinstance(tile, int):
            return slice(tile * TILE, (tile + 1) * TILE)
        return pl.ds(pl.multiple_of(tile * TILE, TILE), TILE)

    def spot(tile):
        return tile % 2 if isinstance(tile, int) else 0

    def standardize(step, tile):
        owner, turn = donor_at(step), turn_of(step)
        lanes = lanes_of(tile)
        coef = beta[owner, :, lanes].astype(jnp.int32).astype(jnp.float32)
        coef = coef * beta_sides[owner, 1:2, lanes] * narrow
        scale = beta_sides[owner, 0:1, lanes]
        for piece in range(3):
            rounded = coef.astype(jnp.bfloat16)
            pieces[spot(tile), piece * K : (piece + 1) * K, :] = rounded
            coef = coef - rounded.astype(jnp.float32)
        for first in range(0, don_rows, STRIP):
            rows = slice(first, first + STRIP)
            fitted = jnp.dot(ccc[rows, 0 : 3 * K], pieces[spot(tile)], preferred_element_type=jnp.float32)
            part = xv[turn, rows, lanes].astype(jnp.float32)
            xv[turn, rows, lanes] = (part * scale - fitted).astype(jnp.bfloat16)

    def pick(step, tile):
        owner, turn = donor_at(step), turn_of(step)
        lanes = lanes_of(tile)
        found = jnp.dot(expr_t[...], xv[turn, :, lanes], preferred_element_type=jnp.float32)
        for side in range(TILE // VB):
            wide[2 * spot(tile) + side, PAD : PAD + genes_all, :] = found[:, side * VB : (side + 1) * VB]
        for side in range(TILE // VB):
            block = tile * (TILE // VB) + side
            place = place_ref[owner * (cols // VB) + block]
            base = jnp.right_shift(place - LEAD, 2) + PAD
            found = wide[2 * spot(tile) + side, pl.ds(base, 16), :]
            if step:
                slot_out[step, block] = found
            else:
                slot_in[my_donor, block] = found

    each(0, tiles, lambda tile: standardize(0, tile))

    each(1, groups, lambda step: slab_back(step).wait_recv())
    per_copy = 4

    def unfold(index, carry):
        first = pl.multiple_of(index * per_copy, per_copy)
        part = slab[pl.ds(first, per_copy)].astype(jnp.float32)
        rows = pl.ds(pl.multiple_of(first * 8, per_copy * 8), per_copy * 8)
        expr_t[rows, 0:half] = part[:, 0:8, :].reshape(per_copy * 8, half).astype(jnp.bfloat16)
        expr_t[rows, half : 2 * half] = (
            part[:, 8:16, :].reshape(per_copy * 8, half).astype(jnp.bfloat16)
        )
        return carry

    lax.fori_loop(0, groups // per_copy, unfold, 0)
    each(1, groups, lambda step: coef_back(step).wait_recv())
    expr_coef = expr_sums[...].reshape(genes_all, 128)
    expr_scale = expr_coef[:, K : K + 1]
    expr_coef = jnp.where(iota((genes_all, 128), 1) < K, expr_coef, 0.0)
    expr_pieces = []
    for piece in range(3):
        rounded = expr_coef.astype(jnp.bfloat16)
        expr_pieces.append(rounded)
        expr_coef = expr_coef - rounded.astype(jnp.float32)
    for first in range(0, don_rows, STRIP):
        lanes = slice(first, first + STRIP)
        resid = expr_t[:, lanes].astype(jnp.float32)
        for part in expr_pieces:
            resid = resid - jnp.dot(part, ct[:, lanes], preferred_element_type=jnp.float32)
        expr_t[:, lanes] = (resid * expr_scale).astype(jnp.bfloat16)

    each(0, tiles, lambda tile: pick(0, tile))
    for step in (1, 3, 2):
        from_donor(step, beta, beta_sent, beta_got).wait_recv()
        from_donor(step, beta_sides, scale_sent, scale_got).wait_recv()

        standardize(step, 0)
        for tile in range(tiles):
            if tile + 1 < tiles:
                standardize(step, tile + 1)
            pick(step, tile)
        to_donor(step, slot_out.at[step], slot_in, slot_sent, slot_got).start()

    for step in range(1, donors):
        from_donor(step, slot_in, slot_sent, slot_got).wait_recv()
    donors_all = don_rows * donors
    starts, counts = start_ref[...], count_ref[...]
    gene_row = iota((16, genes_all), 1)
    slot_row = iota((16, genes_all), 0)
    gene_part = jnp.zeros((1, genes_all), jnp.float32)
    for block in range(slot_in.shape[1]):
        total = slot_in[0, block]
        for donor in range(1, donors):
            total = total + slot_in[donor, block]
        terms = jnp.sum(
            cauchy_terms(total * math.sqrt(donors_all - K - 2)), axis=1, keepdims=True
        )
        place = place_ref[my_donor * slot_in.shape[1] + block]
        base = jnp.right_shift(place - LEAD, 2)
        live = (starts <= place) & (place < starts + counts)
        here = (gene_row == slot_row + base) & (slot_row < GMAX)
        column = jnp.sum(jnp.where(here, terms, 0.0), axis=0, keepdims=True)
        gene_part = gene_part + jnp.where(live, column, 0.0)

    near_count, far_count = donors * 2, groups // 2
    my_near = my_donor * 2 + my_core

    def near_id(step):
        place = lax.rem(my_near + step, near_count)
        return place, (lax.div(place, 2), my_chip * 2 + lax.rem(place, 2))

    def far_id(step):
        place = lax.rem(my_chip + step, far_count)
        return place, (my_donor, place * 2 + my_core)

    tail = []
    for buffer, mine, count, where, sent, got in (
        (near, my_near, near_count, near_id, near_sent, near_got),
        (far, my_chip, far_count, far_id, far_sent, far_got),
    ):
        buffer[mine] = gene_part
        for step in range(1, count):
            copy = pltpu.make_async_remote_copy(
                src_ref=buffer.at[mine],
                dst_ref=buffer.at[mine],
                send_sem=sent.at[step],
                recv_sem=got.at[mine],
                device_id=where(step)[1],
                device_id_type=MESH,
            )
            copy.start()
            tail.append(copy)
        for step in range(1, count):
            peer, device = where(step)
            pltpu.make_async_remote_copy(
                src_ref=buffer.at[peer],
                dst_ref=buffer.at[peer],
                send_sem=sent.at[step],
                recv_sem=got.at[peer],
                device_id=device,
                device_id_type=MESH,
            ).wait_recv()
        gene_part = buffer[0]
        for index in range(1, count):
            gene_part = gene_part + buffer[index]

    covered = jnp.minimum(starts + counts, total_blocks) - jnp.maximum(starts, 0)
    gene_stat = gene_part / (VB * covered).astype(jnp.float32)
    gene_value = 0.5 - arctan(gene_stat) / math.pi
    own_gene = iota((genes_here, genes_all), 1) == iota((genes_here, genes_all), 0) + my_var * genes_here
    gene_ref[...] = jnp.broadcast_to(
        jnp.sum(jnp.where(own_gene, gene_value, 0.0), axis=1, keepdims=True), gene_ref.shape
    )
    own_member.wait()
    each(1, groups, lambda step: member_back(step).wait_recv())
    members = members_ref[...]
    path_sum = jnp.dot(
        jnp.broadcast_to(gene_stat, (8, genes_all)),
        members,
        precision=HIGHEST,
        preferred_element_type=jnp.float32,
    )
    path_weight = jnp.sum(members, axis=0, keepdims=True)
    path_ref[...] = (
        0.5 - arctan(path_sum[0:1, :] / jnp.maximum(path_weight, 1.0)) / math.pi
    )
    each(1, groups, lambda step: member_copy(step).wait_send())
    each(1, groups, lambda step: slab_copy(step).wait_send())
    each(1, groups, lambda step: coef_copy(step).wait_send())
    for step in range(1, donors):
        to_donor(step, small.at[my_donor], small, small_sent, small_got).wait_send()
        for copy in (*send_cross(step - 1), *send_beta(step)):
            copy.wait_send()
        to_donor(step, slot_out.at[step], slot_in, slot_sent, slot_got).wait_send()
    for copy in tail:
        copy.wait_send()


def local(genotype, block_place, expression, covariates, gene_start, gene_count, membership):
    don_rows, var_cols = genotype.shape
    blocks_here = block_place.shape[0]
    genes_all = gene_start.shape[0]
    genes_here = expression.shape[1]
    groups = lax.axis_size("var")
    donors = lax.axis_size("donor")
    total_blocks = blocks_here * groups
    paths_here = membership.shape[1] // groups
    cols = var_cols // donors
    blocks_own = blocks_here // donors

    vmem = pl.BlockSpec(memory_space=pltpu.VMEM)
    anywhere = pl.BlockSpec(memory_space=pl.ANY)
    dma = pltpu.SemaphoreType.DMA

    def body(*refs):
        correlate(donors, groups, total_blocks, *refs)

    gene_value, path_value = pl.pallas_call(
        body,
        out_shape=(
            jax.ShapeDtypeStruct((genes_here, 128), jnp.float32),
            jax.ShapeDtypeStruct((1, paths_here), jnp.float32),
        ),
        in_specs=[vmem, vmem, pl.BlockSpec(memory_space=pltpu.SMEM), vmem, vmem, anywhere, anywhere],
        out_specs=(vmem, vmem),
        scratch_shapes=[
            pltpu.VMEM((genes_all, paths_here), jnp.float32),
            pltpu.VMEM((donors, don_rows, cols), jnp.bfloat16),
            pltpu.VMEM((128, don_rows), jnp.bfloat16),
            pltpu.VMEM((don_rows, 256), jnp.bfloat16),
            pltpu.VMEM((donors, ROWS, 128), jnp.float32),
            pltpu.VMEM((K, 128), jnp.float32),
            pltpu.VMEM((donors, K, cols), jnp.int16),
            pltpu.VMEM((donors, 8, cols), jnp.float32),
            pltpu.VMEM((donors, K, cols), jnp.int16),
            pltpu.VMEM((donors, 8, cols), jnp.float32),
            pltpu.VMEM((donors, K, cols), jnp.int16),
            pltpu.VMEM((donors, 8, cols), jnp.float32),
            pltpu.VMEM((groups, 16, don_rows // 2), jnp.bfloat16),
            pltpu.VMEM((genes_all, don_rows), jnp.bfloat16),
            pltpu.VMEM((groups, genes_here, 128), jnp.float32),
            pltpu.VMEM((2, 3 * K, TILE), jnp.bfloat16),
            pltpu.VMEM((2 * (TILE // VB), genes_all + 24, VB), jnp.float32),
            pltpu.VMEM((donors, blocks_own, 16, VB), jnp.float32),
            pltpu.VMEM((donors, blocks_own, 16, VB), jnp.float32),
            pltpu.VMEM((donors * 2, 1, genes_all), jnp.float32),
            pltpu.VMEM((groups // 2, 1, genes_all), jnp.float32),
            *[dma((donors,)) for _ in range(13)],
            *[dma((groups,)) for _ in range(6)],
            dma,
            *[dma((donors * 2,)) for _ in range(2)],
            *[dma((groups // 2,)) for _ in range(2)],
        ],
        compiler_params=pltpu.CompilerParams(
            collective_id=0, has_side_effects=True, vmem_limit_bytes=56 * 2**20
        ),
        name="correlate",
    )(
        covariates.T,
        expression.T,
        block_place,
        gene_start.reshape(1, genes_all),
        gene_count.reshape(1, genes_all),
        genotype,
        membership,
    )

    return (gene_value[:, 0], path_value[0])


def solution(mesh):
    placed = (
        P("donor", "var"),
        P("var"),
        P("donor", "var"),
        P("donor", None),
        P(),
        P(),
        P("var", None),
    )
    return jax.shard_map(
        local, mesh=mesh, in_specs=placed, out_specs=(P("var"), P("var")), check_vma=False
    )
```
